32 devices in a mesh: job: 2 (over y), dp: 1, expert: 16 (over z, x, core).
Axes of the slice: x: 2, y: 2, z: 4, core: 2. Of those that a mesh axis runs over, the one named last changes fastest.
Arguments:
- routes: int32 [512, 8], P(('job', 'dp', 'expert')), parts along dimension 0, may hold values from 0 to 15, all different within a row; in each aligned block of 16 rows (0 to 15, 16 to 31, ...) at most 12 rows name the same one
- gates: float32 [512, 8], P(('job', 'dp', 'expert')), parts along dimension 0, may hold values from 0.05 to 0.45
- grad_out: bfloat16 [512, 3584], P(('job', 'dp', 'expert')), parts along dimension 0, may hold values from -6 to 6
- hidden: bfloat16 [16, 2, 192, 1024], P('expert', ('job', 'dp')), parts along dimension 1, may hold values from -0.59765625 to 0.59765625
- down_weight: bfloat16 [16, 1024, 3584], P('expert', 'dp'), may hold values from -0.1875 to 0.1875
- adapter_a: bfloat16 [32, 16, 1024], P(('job', 'expert')), parts along dimension 0, may hold values from -1.5 to 1.5
- adapter_b: bfloat16 [32, 16, 3584], P(('job', 'expert')), parts along dimension 0, may hold values from -0.09375 to 0.09375
Outputs:
- grad_hidden: bfloat16 [16, 2, 192, 1024], P('expert', ('job', 'dp')), parts along dimension 1
- grad_gates: float32 [512, 8], P(('job', 'dp', 'expert')), parts along dimension 0
- grad_a: float32 [32, 16, 1024], P(('job', 'expert')), parts along dimension 0
- grad_b: float32 [32, 16, 3584], P(('job', 'expert')), parts along dimension 0
The draws below stay inside these ranges and needn't reach their ends.
There are 2 independent parts, one for each index of `job`. The reference program is written for one: setup_inputs(seed, part) draws one part's arguments, and reference() takes and returns one part's arrays. A program takes and returns all parts, laid end to end along the dimension named above; an argument that names none is the same for every part. Nothing has to cross between parts.
Inputs may be any that keep to these rules, and one draw needn't show every extreme that they name: `routes`: each row names 8 different experts. Among the rows of one device no expert is named more than 12 times, a bound that some block reaches there in some devices.
All inputs are finite; a program needn't handle non-finite values.
Results may differ from the reference program's by a relative error of at most 0.015.
Values may be sent and summed in bfloat16 or wider, within the bound.
A program may use at most 64 MiB of HBM per device.

```python
import math
import jax
import jax.numpy as jnp
import numpy as np
from jax import lax

D = 3584
H = 1024
RANK = 16
TOPK = 8
TOK_DEV = 16
EXPERTS = 16
GROUPS = 1
CAP = 12
SLOTS = 192
TOKENS = 256


def block_levels(rng, dims, shards, smallest, top_value):
    level = 1.0
    for dim, shards_of in shards:
        draws = jax.random.uniform(jax.random.fold_in(jax.random.fold_in(rng, 6), dim), (shards_of,), jnp.float32, smallest / len(shards), top_value / len(shards))
        level = level * jnp.repeat(jnp.exp(draws), dims[dim] // shards_of).reshape((-1,) + (1,) * (len(dims) - 1 - dim))
    return level


def routed_block(key, own, number, rows, number_of, top, most, slope):
    order = jax.random.permutation(key, number_of)
    heavy_load, ordinary = load_shares(number_of, rows * top, most, slope, True), load_shares(number_of, rows * top, most, slope, False)
    places = jnp.arange(number_of)

    def named(sizes, offset_by):
        used = int((sizes > 0).sum())
        fixed = max(1, used // 4)
        shifted = fixed + (places - fixed + offset_by * (used - fixed)) % max(1, number_of - fixed)
        return jnp.zeros((number_of,), jnp.int32).at[order[jnp.where(places < fixed, places, shifted)]].set(jnp.asarray(sizes, jnp.int32))

    sizes = jnp.where(number % 4 == 0, named(heavy_load, number // 4), named(ordinary, number - number // 4 - 1))
    mixed = jax.random.permutation(jax.random.fold_in(own, 3), number_of)
    giver, receiver = mixed[0:number_of // 2 * 2:2], mixed[1:number_of // 2 * 2:2]
    slack = jnp.minimum(sizes[giver] - 1, most - sizes[receiver]) // 2
    slack = jnp.where((giver == order[0]) | (receiver == order[0]) | (sizes[receiver] == 0), 0, jnp.maximum(slack, 0))
    shifted = jax.random.randint(jax.random.fold_in(own, 4), (number_of // 2,), 0, 1 << 20) % (slack + 1)
    sizes = sizes.at[giver].add(-shifted).at[receiver].add(shifted)
    labels = jnp.searchsorted(jnp.cumsum(sizes), jnp.arange(rows * top), side="right").astype(jnp.int32)
    grid = labels.reshape(top, rows).T
    grid = grid[jax.random.permutation(jax.random.fold_in(own, 1), rows)]
    offset_by = jax.random.randint(jax.random.fold_in(own, 2), (rows, 1), 0, top)
    return jnp.take_along_axis(grid, (jnp.arange(top)[None, :] + offset_by) % top, axis=1)


def load_shares(number_of, total, reach, lean, full):
    loads = [(1 << 20) // math.isqrt(rank ** lean) + 1 for rank in range(1, number_of + 1)]
    largest = reach if full else min(reach, max(-(-total // number_of), total * loads[0] // sum(loads)))
    least = 1 if total - largest >= number_of - 1 else 0
    holding, rest = [largest] + [least] * (number_of - 1), total - largest - least * (number_of - 1)
    while rest > 0:
        candidates = [i for i in range(1, number_of) if holding[i] < largest] or [i for i in range(1, number_of) if holding[i] < reach]
        pool, remaining = sum([loads[i] for i in candidates]), rest
        for i in candidates:
            more = min(reach - holding[i], max(1, remaining * loads[i] // pool), rest)
            holding[i] = holding[i] + more
            rest = rest - more
    return np.array(holding)


def noise(rng, extent, deviation, most, shards=(), kind=jnp.bfloat16):
    array = jax.random.normal(rng, extent, jnp.float32) * deviation
    if len(shards) > 0:
        array = block_levels(rng, extent, shards, -0.22, 0.18) * array
    return jnp.clip(array, min=-most, max=most).astype(kind)


def setup_inputs(seed: int = 0, part: int = 0) -> dict:
    key_list = jax.random.split(jax.random.key(seed), 8)
    part_splits = jax.random.split(jax.random.fold_in(key_list[7], part), 8)
    routes_keys = jax.random.split(jax.random.fold_in(part_splits[0], 1), TOKENS // TOK_DEV)
    routes_turns = jax.random.permutation(jax.random.fold_in(part_splits[0], 3), TOKENS // TOK_DEV)
    routes = jax.vmap(lambda own, number: routed_block(jax.random.fold_in(part_splits[0], 2), own, number, TOK_DEV, EXPERTS, TOPK, CAP, 2))(routes_keys, routes_turns).reshape((TOKENS, TOPK))
    gates = jnp.clip(0.05 + 0.39999999 * jax.random.uniform(part_splits[1], (TOKENS, TOPK), jnp.float32) ** block_levels(part_splits[1], (TOKENS, TOPK), ((0, 16),), -0.2, 0.2), 0.05, 0.45)
    grad_out = noise(part_splits[2], (TOKENS, D), 1.0, 6.0, ((0, 16),))
    hidden = noise(part_splits[3], (EXPERTS, GROUPS, SLOTS, H), 0.1, 0.59765625, ((0, 16),))
    down_weight = noise(key_list[4], (EXPERTS, H, D), H ** -0.5, 0.1875, ((0, 16),))
    adapter_a = noise(part_splits[5], (EXPERTS, RANK, H), RANK ** -0.5, 1.5, ((0, 16),))
    adapter_b = noise(part_splits[6], (EXPERTS, RANK, D), D ** -0.5, 0.09375, ((0, 16),))
    return {"routes": routes, "gates": gates, "grad_out": grad_out, "hidden": hidden, "down_weight": down_weight, "adapter_a": adapter_a, "adapter_b": adapter_b}


ADAPTER_SCALING = 1.0


def contract_product(left, right, left_dim, right_dim):
    return lax.dot_general(left, right, (((left_dim,), (right_dim,)), ((), ())), preferred_element_type=jnp.float32)


def reference(routes, gates, grad_out, hidden, down_weight, adapter_a, adapter_b):
    blocks = GROUPS * EXPERTS
    per_block = TOK_DEV * TOPK
    chosen = routes.reshape(blocks, per_block)
    onehot = (chosen[:, :, None] == jnp.arange(EXPERTS, dtype=jnp.int32)[None, None, :]).astype(jnp.int32)
    position = jnp.sum((jnp.cumsum(onehot, axis=1) - onehot) * onehot, axis=2)
    block_ids = jnp.broadcast_to(jnp.arange(blocks, dtype=jnp.int32)[:, None], (blocks, per_block))
    group_of = block_ids // EXPERTS
    slot_of = (block_ids % EXPERTS) * CAP + position
    token_ids = block_ids * TOK_DEV + jnp.broadcast_to(jnp.arange(per_block, dtype=jnp.int32)[None, :] // TOPK, (blocks, per_block))
    table_token = jnp.full((EXPERTS, GROUPS, SLOTS), -1, jnp.int32).at[chosen, group_of, slot_of].set(token_ids)
    table_gate = jnp.zeros((EXPERTS, GROUPS, SLOTS), jnp.float32).at[chosen, group_of, slot_of].set(gates.reshape(blocks, per_block))

    def one_expert(expert_items):
        slot_tokens, gate_rows, hidden_slot_rows, weight, adapter_down_factor, factor_b = expert_items
        filled = slot_tokens >= 0
        grad_rows = jnp.where(filled[:, :, None], grad_out[jnp.maximum(slot_tokens, 0)], jnp.zeros((), jnp.bfloat16))
        grad_rows = grad_rows.reshape(GROUPS * SLOTS, D)
        gate_rows = gate_rows.reshape(GROUPS * SLOTS)
        hidden_slot_rows = hidden_slot_rows.reshape(GROUPS * SLOTS, H)
        frozen_gradient_term = contract_product(grad_rows, weight, 1, 1)
        lowrank_backward = contract_product(grad_rows, factor_b, 1, 1)
        passed_gradient = frozen_gradient_term + ADAPTER_SCALING * jnp.dot(lowrank_backward.astype(jnp.bfloat16), adapter_down_factor, preferred_element_type=jnp.float32)
        grad_hid = (gate_rows[:, None] * passed_gradient).astype(jnp.bfloat16)
        slot_dgate = jnp.sum(hidden_slot_rows.astype(jnp.float32) * passed_gradient, axis=1)
        gate_weighted_output = (gate_rows[:, None] * lowrank_backward).astype(jnp.bfloat16)
        gradient_first_factor = ADAPTER_SCALING * contract_product(gate_weighted_output, hidden_slot_rows, 0, 0)
        lowrank_forward = contract_product(hidden_slot_rows, adapter_down_factor, 1, 1).astype(jnp.bfloat16)
        gate_scaled_rows = (gate_rows[:, None] * grad_rows.astype(jnp.float32)).astype(jnp.bfloat16)
        gradient_second_factor = ADAPTER_SCALING * contract_product(lowrank_forward, gate_scaled_rows, 0, 0)
        return grad_hid.reshape(GROUPS, SLOTS, H), slot_dgate.reshape(GROUPS, SLOTS), gradient_first_factor, gradient_second_factor

    grad_hidden, slot_dgate, grad_a, grad_b = lax.map(one_expert, (table_token, table_gate, hidden, down_weight, adapter_a, adapter_b))
    grad_gates = slot_dgate[chosen, group_of, slot_of].reshape(TOKENS, TOPK)
    return grad_hidden, grad_gates, grad_a, grad_b
```

```python
import functools

import jax
import jax.numpy as jnp
from jax import lax
from jax.experimental import pallas as pl
from jax.experimental.pallas import tpu as pltpu
from jax.sharding import PartitionSpec as P

ADAPTER_SCALING = 1.0
MESH = pl.DeviceIdType.MESH


def contract_product(left, right, left_dim, right_dim):
    return lax.dot_general(
        left, right, (((left_dim,), (right_dim,)), ((), ())), preferred_element_type=jnp.float32
    )


def expert_terms(
    frozen_gradient_term,
    grad_rows,
    gate_rows,
    hidden_slot_rows,
    adapter_down_factor,
    factor_b,
    gate_scaled_rows,
):
    lowrank_backward = contract_product(grad_rows, factor_b, 1, 1)
    passed_gradient = frozen_gradient_term + ADAPTER_SCALING * jnp.dot(
        lowrank_backward.astype(jnp.bfloat16),
        adapter_down_factor,
        preferred_element_type=jnp.float32,
    )
    grad_hid = (gate_rows[:, None] * passed_gradient).astype(jnp.bfloat16)
    slot_dgate = jnp.sum(hidden_slot_rows.astype(jnp.float32) * passed_gradient, axis=1)
    gate_weighted_output = (gate_rows[:, None] * lowrank_backward).astype(jnp.bfloat16)
    first_factor_term = ADAPTER_SCALING * contract_product(
        gate_weighted_output, hidden_slot_rows, 0, 0
    )
    lowrank_forward = contract_product(hidden_slot_rows, adapter_down_factor, 1, 1).astype(
        jnp.bfloat16
    )
    second_factor_term = ADAPTER_SCALING * contract_product(lowrank_forward, gate_scaled_rows, 0, 0)
    return (grad_hid, slot_dgate, first_factor_term, second_factor_term)


def shards(routes, gates, grad_out, hidden, down_weight, adapter_a, adapter_b):
    tok_rows, top_count = routes.shape
    experts = lax.axis_size("expert")
    slots = hidden.shape[2]
    capacity = slots // experts
    per_block = tok_rows * top_count
    chosen = routes.reshape(per_block)
    onehot = (chosen[:, None] == jnp.arange(experts, dtype=jnp.int32)[None, :]).astype(jnp.int32)
    position = jnp.sum((jnp.cumsum(onehot, axis=0) - onehot) * onehot, axis=1)
    slot_of = chosen * capacity + position
    placing = slot_of[:, None] == jnp.arange(slots, dtype=jnp.int32)[None, :]
    tok_place = jnp.any(placing.reshape(tok_rows, top_count, slots), axis=1).astype(jnp.bfloat16)
    send_grad = (
        contract_product(tok_place, grad_out, 0, 0)
        .astype(jnp.bfloat16)
        .reshape(experts, capacity, grad_out.shape[1])
    )
    send_gate = jnp.sum(jnp.where(placing, gates.reshape(per_block)[:, None], 0.0), axis=0).reshape(
        experts, capacity
    )
    recv_grad, recv_gate = (
        lax.all_to_all(send_grad, "expert", split_axis=0, concat_axis=0, tiled=True),
        lax.all_to_all(
            send_gate.astype(jnp.bfloat16), "expert", split_axis=0, concat_axis=0, tiled=True
        ).astype(send_gate.dtype),
    )
    grad_rows = recv_grad.reshape(slots, grad_out.shape[1])
    gate_rows = recv_gate.reshape(slots)
    hidden_slot_rows = hidden[0, 0]
    adapter_down_factor = adapter_a[0]
    factor_b = adapter_b[0]
    gate_scaled_rows = (gate_rows[:, None] * grad_rows.astype(jnp.float32)).astype(jnp.bfloat16)
    frozen_gradient_term = contract_product(
        grad_rows, lax.all_gather(down_weight[0], "dp", axis=0, tiled=True), 1, 1
    )
    grad_hid, slot_dgate, first_factor_term, second_factor_term = expert_terms(
        frozen_gradient_term,
        grad_rows,
        gate_rows,
        hidden_slot_rows,
        adapter_down_factor,
        factor_b,
        gate_scaled_rows,
    )
    gradient_first_factor, gradient_second_factor = (
        lax.psum(first_factor_term.astype(jnp.bfloat16), "dp").astype(jnp.float32),
        lax.psum(second_factor_term.astype(jnp.bfloat16), "dp").astype(jnp.float32),
    )
    back_gate = lax.all_to_all(
        slot_dgate.reshape(experts, capacity), "expert", split_axis=0, concat_axis=0, tiled=True
    )
    grad_gates = jnp.sum(
        jnp.where(placing, back_gate.reshape(slots)[None, :], 0.0), axis=1
    ).reshape(tok_rows, top_count)
    return (
        grad_hid[None, None],
        grad_gates,
        gradient_first_factor[None],
        gradient_second_factor[None],
    )


def flip(value, bit):
    return value + bit - 2 * bit * ((value // bit) % 2)


def xor(value, mask):
    bit = 1
    while bit <= mask:
        if mask & bit:
            value = flip(value, bit)
        bit *= 2
    return value


def one_hot(shape, pick):
    rows = lax.broadcasted_iota(jnp.int32, shape, 0)
    columns = lax.broadcasted_iota(jnp.int32, shape, 1)
    return pick(rows, columns).astype(jnp.bfloat16)


def tile_of(size, most):
    tile = most
    while size % tile:
        tile //= 2
    return tile


def fused_kernel(
    experts,
    routes_ref,
    gates_ref,
    grad_ref,
    hidden_ref,
    weight_hbm,
    a_ref,
    b_ref,
    grad_hid_ref,
    grad_gates_ref,
    grad_a_ref,
    grad_b_ref,
    tokens,
    weight,
    rows,
    products,
    back_out,
    back_in,
    weight_sem,
    send_sem,
    recv_sem,
    back_send_sem,
    back_recv_sem,
):
    me = lax.axis_index("expert")
    tok_rows, top_count = routes_ref.shape
    features = grad_ref.shape[1]
    slots, units = hidden_ref.shape
    capacity = slots // experts
    total = experts * tok_rows
    planes = experts // 4
    z, x, core = me // 4, (me // 2) % 2, me % 2
    bf16, f32 = jnp.bfloat16, jnp.float32

    load_weight = pltpu.make_async_copy(weight_hbm, weight, weight_sem)
    load_weight.start()

    barrier = pltpu.get_barrier_semaphore()
    for step in range(1, experts):
        pl.semaphore_signal(
            barrier,
            inc=1,
            device_id={"expert": lax.rem(me + step, experts)},
            device_id_type=MESH,
        )

    tokens[me, :, :features] = grad_ref[...]
    high = gates_ref[...].astype(bf16)
    low = (gates_ref[...] - high.astype(f32)).astype(bf16)
    meta = jnp.zeros((tok_rows, 128), f32)
    for part, values in enumerate((routes_ref[...].astype(f32).astype(bf16), high, low)):
        spread = one_hot((top_count, 128), lambda r, c: c == r + part * top_count)
        meta = meta + contract_product(values, spread, 1, 0)
    tokens[me, :, features:] = meta.astype(bf16)
    pl.semaphore_wait(barrier, experts - 1)

    def index(plane, column, lane):
        return plane * 4 + column * 2 + lane

    x_mate, core_mate = index(z, 1 - x, core), index(z, x, 1 - core)
    sent = []

    def send(shard, target):
        copy = pltpu.make_async_remote_copy(
            src_ref=tokens.at[shard],
            dst_ref=tokens.at[shard],
            send_sem=send_sem.at[len(sent)],
            recv_sem=recv_sem.at[shard],
            device_id={"expert": target},
            device_id_type=MESH,
        )
        copy.start()
        sent.append(copy)

    def arrived(shard):
        pltpu.make_async_remote_copy(
            src_ref=tokens.at[shard],
            dst_ref=tokens.at[shard],
            send_sem=send_sem.at[0],
            recv_sem=recv_sem.at[shard],
            device_id={"expert": core_mate},
            device_id_type=MESH,
        ).wait_recv()

    send(me, x_mate)
    for step in range(1, planes):
        send(me, index(xor(z, step), x, core))
    send(me, core_mate)
    for step in range(planes):
        plane = xor(z, step)
        if step > 0:
            mine = index(plane, x, core)
            arrived(mine)
            send(mine, x_mate)
            send(mine, core_mate)
        if step == planes - 1:
            hidden = hidden_ref[...]
            low_fwd = contract_product(hidden, a_ref[...], 1, 1)
        if step > 0:
            across = index(xor(z, step - 1), 1 - x, core)
            arrived(across)
            send(across, core_mate)
    across = index(xor(z, planes - 1), 1 - x, core)
    arrived(across)
    send(across, core_mate)
    for step in range(planes):
        arrived(index(xor(z, step), x, 1 - core))
        arrived(index(xor(z, step), 1 - x, 1 - core))

    gathered = tokens[:, :, features:].reshape(total, 128)
    eye = one_hot((128, 128), lambda r, c: r == c)
    turned = contract_product(eye, gathered, 1, 1)
    named = turned[:top_count] == me.astype(f32)
    gate_of = jnp.where(
        named, turned[top_count : 2 * top_count] + turned[2 * top_count : 3 * top_count], 0.0
    )
    gate_tok = jnp.sum(gate_of, axis=0, keepdims=True)
    match = jnp.sum(named.astype(f32), axis=0, keepdims=True)
    before = one_hot((total, total), lambda r, c: (r < c) & (r // tok_rows == c // tok_rows))
    position = contract_product(
        jnp.broadcast_to(match, (8, total)).astype(bf16), before, 1, 0
    )[:1]
    block = lax.broadcasted_iota(jnp.int32, (1, total), 1) // tok_rows
    slot_of = jnp.where(match > 0.0, block.astype(f32) * capacity + position, -1.0)
    slot_ids = lax.broadcasted_iota(jnp.int32, (slots, total), 0).astype(f32)
    placing = slot_ids == slot_of
    gate = jnp.sum(jnp.where(placing, gate_tok, 0.0), axis=1, keepdims=True)
    place = placing.astype(bf16)

    wide = tile_of(features, 512)

    @pl.loop(0, features // wide)
    def _(tile):
        columns = pl.ds(pl.multiple_of(tile * wide, wide), wide)
        rows[:, columns] = contract_product(
            place, tokens[:, :, columns].reshape(total, wide), 1, 0
        ).astype(bf16)

    low_back = contract_product(rows[...], b_ref[...], 1, 1)
    low_back_b = low_back.astype(bf16)
    load_weight.wait()
    deep = tile_of(units, 256)
    products[...] = jnp.zeros_like(products)

    @pl.loop(0, units // deep)
    def _(tile):
        span = pl.ds(pl.multiple_of(tile * deep, deep), deep)
        through = contract_product(rows[...], weight[span, :], 1, 1)
        through = through + contract_product(low_back_b, a_ref[:, span], 1, 0)
        grad_hid_ref[:, span] = (gate * through).astype(bf16)
        products[...] += hidden_ref[:, span].astype(f32) * through

    dgate = jnp.sum(products[...], axis=1, keepdims=True)
    dgate_tok = jnp.sum(jnp.where(placing, dgate, 0.0), axis=0, keepdims=True)
    exact = lax.Precision.HIGHEST
    source = lax.broadcasted_iota(jnp.int32, (experts, total), 0)
    owner = lax.broadcasted_iota(jnp.int32, (experts, total), 1) // tok_rows
    by_source = lax.dot_general(
        jnp.where(source == owner, dgate_tok, 0.0),
        one_hot((total, 128), lambda r, c: r % tok_rows == c).astype(f32),
        (((1,), (0,)), ((), ())),
        precision=exact,
        preferred_element_type=f32,
    )
    back_out[...] = jnp.broadcast_to(by_source[:, None, :], back_out.shape)
    returned = []
    for step in range(1, experts):
        target = lax.rem(me + step, experts)
        copy = pltpu.make_async_remote_copy(
            src_ref=back_out.at[target],
            dst_ref=back_in.at[me],
            send_sem=back_send_sem.at[step],
            recv_sem=back_recv_sem.at[me],
            device_id={"expert": target},
            device_id_type=MESH,
        )
        copy.start()
        returned.append(copy)
    back_in[me] = back_out[me]

    weighted = (gate * low_back).astype(bf16)
    grad_a_ref[...] = contract_product(weighted, hidden_ref[...], 0, 0)
    scaled = (gate * low_fwd).astype(bf16)

    @pl.loop(0, features // wide)
    def _(tile):
        columns = pl.ds(pl.multiple_of(tile * wide, wide), wide)
        grad_b_ref[:, columns] = contract_product(scaled, rows[:, columns], 0, 0)

    for copy in sent:
        copy.wait_send()
    for copy in returned:
        copy.wait_send()
    for step in range(1, experts):
        origin = lax.rem(me + step, experts)
        pltpu.make_async_remote_copy(
            src_ref=back_out.at[origin],
            dst_ref=back_in.at[origin],
            send_sem=back_send_sem.at[step],
            recv_sem=back_recv_sem.at[origin],
            device_id={"expert": origin},
            device_id_type=MESH,
        ).wait_recv()
    back = lax.dot_general(
        one_hot((tok_rows, 128), lambda r, c: r == c).astype(f32),
        back_in[:, 0, :],
        (((1,), (1,)), ((), ())),
        precision=exact,
        preferred_element_type=f32,
    )
    chosen = routes_ref[...]
    picked = jnp.zeros((tok_rows, top_count), f32)
    for expert in range(experts):
        picked = picked + jnp.where(chosen == expert, back[:, expert : expert + 1], 0.0)
    grad_gates_ref[...] = picked


def fused_shards(experts, routes, gates, grad_out, hidden, down_weight, adapter_a, adapter_b):
    tok_rows, top_count = routes.shape
    features = grad_out.shape[1]
    slots, units = hidden.shape[2:]
    vmem = pl.BlockSpec(memory_space=pltpu.VMEM)
    dma = pltpu.SemaphoreType.DMA
    grad_hid, grad_gates, grad_a, grad_b = pl.pallas_call(
        functools.partial(fused_kernel, experts),
        out_shape=(
            jax.ShapeDtypeStruct((slots, units), jnp.bfloat16),
            jax.ShapeDtypeStruct((tok_rows, top_count), jnp.float32),
            jax.ShapeDtypeStruct(adapter_a.shape[1:], jnp.float32),
            jax.ShapeDtypeStruct(adapter_b.shape[1:], jnp.float32),
        ),
        in_specs=[vmem] * 4 + [pl.BlockSpec(memory_space=pl.ANY)] + [vmem] * 2,
        out_specs=(vmem,) * 4,
        scratch_shapes=[
            pltpu.VMEM((experts, tok_rows, features + 128), jnp.bfloat16),
            pltpu.VMEM((units, features), jnp.bfloat16),
            pltpu.VMEM((slots, features), jnp.bfloat16),
            pltpu.VMEM((slots, tile_of(units, 256)), jnp.float32),
            pltpu.VMEM((experts, 8, 128), jnp.float32),
            pltpu.VMEM((experts, 8, 128), jnp.float32),
            dma,
            dma((experts,)),
            dma((experts,)),
            dma((experts,)),
            dma((experts,)),
        ],
        compiler_params=pltpu.CompilerParams(
            collective_id=0, has_side_effects=True, vmem_limit_bytes=56 * 1024 * 1024
        ),
    )(routes, gates, grad_out, hidden[0, 0], down_weight[0], adapter_a[0], adapter_b[0])
    return grad_hid[None, None], grad_gates, grad_a[None], grad_b[None]


def solution(mesh):
    placed = (
        P(("job", "dp", "expert"), None),
        P(("job", "dp", "expert"), None),
        P(("job", "dp", "expert"), None),
        P("expert", ("job", "dp"), None, None),
        P("expert", "dp", None),
        P(("job", "expert"), None, None),
        P(("job", "expert"), None, None),
    )
    experts = mesh.shape["expert"]
    fused = mesh.shape["dp"] == 1 and experts in (8, 16)
    return jax.shard_map(
        functools.partial(fused_shards, experts) if fused else shards,
        mesh=mesh,
        in_specs=placed,
        out_specs=(
            P("expert", ("job", "dp"), None, None),
            P(("job", "dp", "expert"), None),
            P(("job", "expert"), None, None),
            P(("job", "expert"), None, None),
        ),
        check_vma=False,
    )
```

```python
import functools

import jax
import jax.numpy as jnp
from jax import lax
from jax.experimental import pallas as pl
from jax.experimental.pallas import tpu as pltpu
from jax.sharding import PartitionSpec as P

ADAPTER_SCALING = 1.0
MESH = pl.DeviceIdType.MESH
CHUNKS = 2


def contract_product(left, right, left_dim, right_dim):
    return lax.dot_general(
        left, right, (((left_dim,), (right_dim,)), ((), ())), preferred_element_type=jnp.float32
    )


def expert_terms(
    frozen_gradient_term,
    grad_rows,
    gate_rows,
    hidden_slot_rows,
    adapter_down_factor,
    factor_b,
    gate_scaled_rows,
):
    lowrank_backward = contract_product(grad_rows, factor_b, 1, 1)
    passed_gradient = frozen_gradient_term + ADAPTER_SCALING * jnp.dot(
        lowrank_backward.astype(jnp.bfloat16),
        adapter_down_factor,
        preferred_element_type=jnp.float32,
    )
    grad_hid = (gate_rows[:, None] * passed_gradient).astype(jnp.bfloat16)
    slot_dgate = jnp.sum(hidden_slot_rows.astype(jnp.float32) * passed_gradient, axis=1)
    gate_weighted_output = (gate_rows[:, None] * lowrank_backward).astype(jnp.bfloat16)
    first_factor_term = ADAPTER_SCALING * contract_product(
        gate_weighted_output, hidden_slot_rows, 0, 0
    )
    lowrank_forward = contract_product(hidden_slot_rows, adapter_down_factor, 1, 1).astype(
        jnp.bfloat16
    )
    second_factor_term = ADAPTER_SCALING * contract_product(lowrank_forward, gate_scaled_rows, 0, 0)
    return (grad_hid, slot_dgate, first_factor_term, second_factor_term)


def shards(routes, gates, grad_out, hidden, down_weight, adapter_a, adapter_b):
    tok_rows, top_count = routes.shape
    experts = lax.axis_size("expert")
    slots = hidden.shape[2]
    capacity = slots // experts
    per_block = tok_rows * top_count
    chosen = routes.reshape(per_block)
    onehot = (chosen[:, None] == jnp.arange(experts, dtype=jnp.int32)[None, :]).astype(jnp.int32)
    position = jnp.sum((jnp.cumsum(onehot, axis=0) - onehot) * onehot, axis=1)
    slot_of = chosen * capacity + position
    placing = slot_of[:, None] == jnp.arange(slots, dtype=jnp.int32)[None, :]
    tok_place = jnp.any(placing.reshape(tok_rows, top_count, slots), axis=1).astype(jnp.bfloat16)
    send_grad = (
        contract_product(tok_place, grad_out, 0, 0)
        .astype(jnp.bfloat16)
        .reshape(experts, capacity, grad_out.shape[1])
    )
    send_gate = jnp.sum(jnp.where(placing, gates.reshape(per_block)[:, None], 0.0), axis=0).reshape(
        experts, capacity
    )
    recv_grad, recv_gate = (
        lax.all_to_all(send_grad, "expert", split_axis=0, concat_axis=0, tiled=True),
        lax.all_to_all(
            send_gate.astype(jnp.bfloat16), "expert", split_axis=0, concat_axis=0, tiled=True
        ).astype(send_gate.dtype),
    )
    grad_rows = recv_grad.reshape(slots, grad_out.shape[1])
    gate_rows = recv_gate.reshape(slots)
    hidden_slot_rows = hidden[0, 0]
    adapter_down_factor = adapter_a[0]
    factor_b = adapter_b[0]
    gate_scaled_rows = (gate_rows[:, None] * grad_rows.astype(jnp.float32)).astype(jnp.bfloat16)
    frozen_gradient_term = contract_product(
        grad_rows, lax.all_gather(down_weight[0], "dp", axis=0, tiled=True), 1, 1
    )
    grad_hid, slot_dgate, first_factor_term, second_factor_term = expert_terms(
        frozen_gradient_term,
        grad_rows,
        gate_rows,
        hidden_slot_rows,
        adapter_down_factor,
        factor_b,
        gate_scaled_rows,
    )
    gradient_first_factor, gradient_second_factor = (
        lax.psum(first_factor_term.astype(jnp.bfloat16), "dp").astype(jnp.float32),
        lax.psum(second_factor_term.astype(jnp.bfloat16), "dp").astype(jnp.float32),
    )
    back_gate = lax.all_to_all(
        slot_dgate.reshape(experts, capacity), "expert", split_axis=0, concat_axis=0, tiled=True
    )
    grad_gates = jnp.sum(
        jnp.where(placing, back_gate.reshape(slots)[None, :], 0.0), axis=1
    ).reshape(tok_rows, top_count)
    return (
        grad_hid[None, None],
        grad_gates,
        gradient_first_factor[None],
        gradient_second_factor[None],
    )


def flip(value, bit):
    return value + bit - 2 * bit * ((value // bit) % 2)


def xor(value, mask):
    bit = 1
    while bit <= mask:
        if mask & bit:
            value = flip(value, bit)
        bit *= 2
    return value


def one_hot(shape, pick):
    rows = lax.broadcasted_iota(jnp.int32, shape, 0)
    columns = lax.broadcasted_iota(jnp.int32, shape, 1)
    return pick(rows, columns).astype(jnp.bfloat16)


def tile_of(size, most):
    tile = most
    while size % tile:
        tile //= 2
    return tile


def fused_kernel(
    experts,
    routes_ref,
    gates_ref,
    grad_ref,
    hidden_ref,
    weight_hbm,
    a_ref,
    b_ref,
    grad_hid_ref,
    grad_gates_ref,
    grad_a_ref,
    grad_b_ref,
    meta_tokens,
    tokens,
    weight,
    rows,
    through_sum,
    before,
    back_out,
    back_in,
    weight_sem,
    send_sem,
    recv_sem,
    back_send_sem,
    back_recv_sem,
):
    me = lax.axis_index("expert")
    top_count, tok_rows = routes_ref.shape
    chunks = tokens.shape[0] + 1
    chunk = tokens.shape[3]
    slots, units = hidden_ref.shape
    capacity = slots // experts
    total = experts * tok_rows
    planes = experts // 4
    z, x, core = me // 4, (me // 2) % 2, me % 2
    bf16, f32 = jnp.bfloat16, jnp.float32

    load_weight = pltpu.make_async_copy(weight_hbm, weight, weight_sem)
    load_weight.start()

    barrier = pltpu.get_barrier_semaphore()
    for step in range(1, experts):
        pl.semaphore_signal(
            barrier,
            inc=1,
            device_id={"expert": lax.rem(me + step, experts)},
            device_id_type=MESH,
        )

    def held(part, shard):
        return meta_tokens.at[shard] if part == 0 else tokens.at[part - 1, shard]

    meta_tokens[me, :, :chunk] = grad_ref[:, :chunk]
    for part in range(1, chunks):
        tokens[part - 1, me] = grad_ref[:, part * chunk : (part + 1) * chunk]
    high = gates_ref[...].astype(bf16)
    low = (gates_ref[...] - high.astype(f32)).astype(bf16)
    meta = jnp.zeros((tok_rows, 128), f32)
    for part, values in enumerate((routes_ref[...].astype(f32).astype(bf16), high, low)):
        spread = one_hot((top_count, 128), lambda r, c: c == r + part * top_count)
        meta = meta + contract_product(values, spread, 0, 0)
    meta_tokens[me, :, chunk:] = meta.astype(bf16)
    pl.semaphore_wait(barrier, experts - 1)

    def index(plane, column, lane):
        return plane * 4 + column * 2 + lane

    x_mate, core_mate = index(z, 1 - x, core), index(z, x, 1 - core)
    sent = []

    def send(part, shard, target):
        copy = pltpu.make_async_remote_copy(
            src_ref=held(part, shard),
            dst_ref=held(part, shard),
            send_sem=send_sem.at[len(sent)],
            recv_sem=recv_sem.at[part, shard],
            device_id={"expert": target},
            device_id_type=MESH,
        )
        copy.start()
        sent.append(copy)

    def arrived(part, shard):
        pltpu.make_async_remote_copy(
            src_ref=held(part, shard),
            dst_ref=held(part, shard),
            send_sem=send_sem.at[0],
            recv_sem=recv_sem.at[part, shard],
            device_id={"expert": core_mate},
            device_id_type=MESH,
        ).wait_recv()

    for part in range(chunks):
        send(part, me, x_mate)
        for step in range(1, planes):
            send(part, me, index(xor(z, step), x, core))
        send(part, me, core_mate)

    before[...] = one_hot(
        (total, total), lambda r, c: (r < c) & (lax.div(r, tok_rows) == lax.div(c, tok_rows))
    )
    low_fwd = contract_product(hidden_ref[...], a_ref[...], 1, 1)
    state = {}
    deep = tile_of(units, 256)

    def core_arrived(part):
        for step in range(planes):
            arrived(part, index(xor(z, step), x, 1 - core))
            arrived(part, index(xor(z, step), 1 - x, 1 - core))

    def route():
        gathered = meta_tokens[:, :, chunk:].reshape(total, 128)
        eye = one_hot((128, 128), lambda r, c: r == c)
        turned = contract_product(eye, gathered, 1, 1)
        named = turned[:top_count] == me.astype(f32)
        gate_of = jnp.where(
            named, turned[top_count : 2 * top_count] + turned[2 * top_count : 3 * top_count], 0.0
        )
        gate_tok = jnp.sum(gate_of, axis=0, keepdims=True)
        match = jnp.sum(named.astype(f32), axis=0, keepdims=True)
        position = contract_product(
            jnp.broadcast_to(match, (8, total)).astype(bf16), before[...], 1, 0
        )[:1]
        block = lax.div(lax.broadcasted_iota(jnp.int32, (1, total), 1), tok_rows)
        slot_of = jnp.where(match > 0.0, block.astype(f32) * capacity + position, -1.0)
        slot_ids = lax.broadcasted_iota(jnp.int32, (slots, total), 0).astype(f32)
        placing = slot_ids == slot_of
        state["slot_of"] = slot_of
        state["gate"] = jnp.sum(jnp.where(placing, gate_tok, 0.0), axis=1, keepdims=True)
        state["place"] = placing.astype(bf16)

    def columns(part):
        return slice(part * chunk, (part + 1) * chunk)

    def place_rows(part):
        source = meta_tokens[:, :, :chunk] if part == 0 else tokens[part - 1]
        rows[:, columns(part)] = contract_product(
            state["place"], source.reshape(total, chunk), 1, 0
        ).astype(bf16)
        low = contract_product(rows[:, columns(part)], b_ref[:, columns(part)], 1, 1)
        state["low_back"] = low if part == 0 else state["low_back"] + low

    def add_product(part, tile):
        span = slice(tile * deep, (tile + 1) * deep)
        product = contract_product(rows[:, columns(part)], weight[span, columns(part)], 1, 1)
        if part == 0:
            through_sum[:, span] = product
        else:
            through_sum[:, span] += product

    def work_on(part):
        def first():
            core_arrived(part)
            if part == 0:
                route()
                load_weight.wait()
            place_rows(part)

        return [first] + [
            functools.partial(add_product, part, tile) for tile in range(units // deep)
        ]

    for part in range(chunks):
        work = work_on(part - 1) if part > 0 else []
        for step in range(planes):
            if step > 0:
                mine = index(xor(z, step), x, core)
                arrived(part, mine)
                send(part, mine, x_mate)
                send(part, mine, core_mate)
            across = index(xor(z, step), 1 - x, core)
            if step < planes - 1:
                arrived(part, across)
                send(part, across, core_mate)
            if work:
                work.pop(0)()
        while work:
            work.pop(0)()
        across = index(xor(z, planes - 1), 1 - x, core)
        arrived(part, across)
        send(part, across, core_mate)
    last = chunks - 1
    core_arrived(last)
    place_rows(last)

    gate, low_back = state["gate"], state["low_back"]
    low_back_b = low_back.astype(bf16)
    dgate = jnp.zeros((slots, 1), f32)
    for tile in range(units // deep):
        span = slice(tile * deep, (tile + 1) * deep)
        through = through_sum[:, span] + contract_product(
            rows[:, columns(last)], weight[span, columns(last)], 1, 1
        )
        through = through + contract_product(low_back_b, a_ref[:, span], 1, 0)
        grad_hid_ref[:, span] = (gate * through).astype(bf16)
        dgate = dgate + jnp.sum(hidden_ref[:, span].astype(f32) * through, axis=1, keepdims=True)

    slot_ids = lax.broadcasted_iota(jnp.int32, (slots, total), 0).astype(f32)
    dgate_tok = jnp.sum(
        jnp.where(slot_ids == state["slot_of"], dgate, 0.0), axis=0, keepdims=True
    )
    exact = lax.Precision.HIGHEST
    source = lax.broadcasted_iota(jnp.int32, (experts, total), 0)
    owner = lax.div(lax.broadcasted_iota(jnp.int32, (experts, total), 1), tok_rows)
    by_source = lax.dot_general(
        jnp.where(source == owner, dgate_tok, 0.0),
        one_hot((total, 128), lambda r, c: lax.rem(r, tok_rows) == c).astype(f32),
        (((1,), (0,)), ((), ())),
        precision=exact,
        preferred_element_type=f32,
    )
    back_out[...] = jnp.broadcast_to(by_source[:, None, :], back_out.shape)
    returned = []
    for step in range(1, experts):
        target = lax.rem(me + step, experts)
        copy = pltpu.make_async_remote_copy(
            src_ref=back_out.at[target],
            dst_ref=back_in.at[me],
            send_sem=back_send_sem.at[step],
            recv_sem=back_recv_sem.at[me],
            device_id={"expert": target},
            device_id_type=MESH,
        )
        copy.start()
        returned.append(copy)
    back_in[me] = back_out[me]

    weighted = (gate * low_back).astype(bf16)
    grad_a_ref[...] = contract_product(weighted, hidden_ref[...], 0, 0)
    scaled = (gate * low_fwd).astype(bf16)
    for part in range(chunks):
        grad_b_ref[:, columns(part)] = contract_product(scaled, rows[:, columns(part)], 0, 0)

    for copy in sent:
        copy.wait_send()
    for copy in returned:
        copy.wait_send()
    for step in range(1, experts):
        origin = lax.rem(me + step, experts)
        pltpu.make_async_remote_copy(
            src_ref=back_out.at[origin],
            dst_ref=back_in.at[origin],
            send_sem=back_send_sem.at[step],
            recv_sem=back_recv_sem.at[origin],
            device_id={"expert": origin},
            device_id_type=MESH,
        ).wait_recv()
    back = lax.dot_general(
        back_in[:, 0, :],
        one_hot((128, tok_rows), lambda r, c: r == c).astype(f32),
        (((1,), (0,)), ((), ())),
        precision=exact,
        preferred_element_type=f32,
    )
    chosen = routes_ref[...]
    picked = jnp.zeros((top_count, tok_rows), f32)
    for expert in range(experts):
        picked = picked + jnp.where(chosen == expert, back[expert : expert + 1, :], 0.0)
    grad_gates_ref[...] = picked


def copy_kernel(*refs):
    count = (len(refs) - 1) // 2
    sems = refs[-1]
    copies = [
        pltpu.make_async_copy(refs[i], refs[count + i], sems.at[i]) for i in range(count)
    ]
    for copy in copies:
        copy.start()
    for copy in copies:
        copy.wait()


def fused_shards(experts, routes, gates, grad_out, hidden, down_weight, adapter_a, adapter_b):
    tok_rows, top_count = routes.shape
    features = grad_out.shape[1]
    slots, units = hidden.shape[2:]
    chunks = CHUNKS
    while features % (chunks * 128):
        chunks -= 1
    chunk = features // chunks
    vmem = pl.BlockSpec(memory_space=pltpu.VMEM)
    hbm = pl.BlockSpec(memory_space=pl.ANY)
    dma = pltpu.SemaphoreType.DMA
    out_shape = (
        jax.ShapeDtypeStruct((slots, units), jnp.bfloat16),
        jax.ShapeDtypeStruct((top_count, tok_rows), jnp.float32),
        jax.ShapeDtypeStruct(adapter_a.shape[1:], jnp.float32),
        jax.ShapeDtypeStruct(adapter_b.shape[1:], jnp.float32),
    )
    results = pl.pallas_call(
        functools.partial(fused_kernel, experts),
        out_shape=out_shape,
        in_specs=[vmem] * 4 + [hbm] + [vmem] * 2,
        out_specs=(vmem,) * 4,
        scratch_shapes=[
            pltpu.VMEM((experts, tok_rows, chunk + 128), jnp.bfloat16),
            pltpu.VMEM((chunks - 1, experts, tok_rows, chunk), jnp.bfloat16),
            pltpu.VMEM((units, features), jnp.bfloat16),
            pltpu.VMEM((slots, features), jnp.bfloat16),
            pltpu.VMEM((slots, units), jnp.float32),
            pltpu.VMEM((experts * tok_rows, experts * tok_rows), jnp.bfloat16),
            pltpu.VMEM((experts, 8, 128), jnp.float32),
            pltpu.VMEM((experts, 8, 128), jnp.float32),
            dma,
            dma((chunks * (experts - 1),)),
            dma((chunks, experts)),
            dma((experts,)),
            dma((experts,)),
        ],
        compiler_params=pltpu.CompilerParams(
            collective_id=0, has_side_effects=True, vmem_limit_bytes=56 * 1024 * 1024
        ),
    )(routes.T, gates.T, grad_out, hidden[0, 0], down_weight[0], adapter_a[0], adapter_b[0])
    grad_hid, grad_gates, grad_a, grad_b = pl.pallas_call(
        copy_kernel,
        out_shape=out_shape,
        in_specs=[hbm] * 4,
        out_specs=(hbm,) * 4,
        scratch_shapes=[dma((4,))],
        compiler_params=pltpu.CompilerParams(vmem_limit_bytes=60 * 1024 * 1024),
    )(*results)
    return grad_hid[None, None], grad_gates.T, grad_a[None], grad_b[None]


def solution(mesh):
    placed = (
        P(("job", "dp", "expert"), None),
        P(("job", "dp", "expert"), None),
        P(("job", "dp", "expert"), None),
        P("expert", ("job", "dp"), None, None),
        P("expert", "dp", None),
        P(("job", "expert"), None, None),
        P(("job", "expert"), None, None),
    )
    experts = mesh.shape["expert"]
    fused = mesh.shape["dp"] == 1 and experts in (8, 16)
    return jax.shard_map(
        functools.partial(fused_shards, experts) if fused else shards,
        mesh=mesh,
        in_specs=placed,
        out_specs=(
            P("expert", ("job", "dp"), None, None),
            P(("job", "dp", "expert"), None),
            P(("job", "expert"), None, None),
            P(("job", "expert"), None, None),
        ),
        check_vma=False,
    )
```

```python
import functools

import jax
import jax.numpy as jnp
from jax import lax
from jax.experimental import pallas as pl
from jax.experimental.pallas import tpu as pltpu
from jax.sharding import PartitionSpec as P

ADAPTER_SCALING = 1.0
MESH = pl.DeviceIdType.MESH


def contract_product(left, right, left_dim, right_dim):
    return lax.dot_general(
        left, right, (((left_dim,), (right_dim,)), ((), ())), preferred_element_type=jnp.float32
    )


def expert_terms(
    frozen_gradient_term,
    grad_rows,
    gate_rows,
    hidden_slot_rows,
    adapter_down_factor,
    factor_b,
    gate_scaled_rows,
):
    lowrank_backward = contract_product(grad_rows, factor_b, 1, 1)
    passed_gradient = frozen_gradient_term + ADAPTER_SCALING * jnp.dot(
        lowrank_backward.astype(jnp.bfloat16),
        adapter_down_factor,
        preferred_element_type=jnp.float32,
    )
    grad_hid = (gate_rows[:, None] * passed_gradient).astype(jnp.bfloat16)
    slot_dgate = jnp.sum(hidden_slot_rows.astype(jnp.float32) * passed_gradient, axis=1)
    gate_weighted_output = (gate_rows[:, None] * lowrank_backward).astype(jnp.bfloat16)
    first_factor_term = ADAPTER_SCALING * contract_product(
        gate_weighted_output, hidden_slot_rows, 0, 0
    )
    lowrank_forward = contract_product(hidden_slot_rows, adapter_down_factor, 1, 1).astype(
        jnp.bfloat16
    )
    second_factor_term = ADAPTER_SCALING * contract_product(lowrank_forward, gate_scaled_rows, 0, 0)
    return (grad_hid, slot_dgate, first_factor_term, second_factor_term)


def shards(routes, gates, grad_out, hidden, down_weight, adapter_a, adapter_b):
    tok_rows, top_count = routes.shape
    experts = lax.axis_size("expert")
    slots = hidden.shape[2]
    capacity = slots // experts
    per_block = tok_rows * top_count
    chosen = routes.reshape(per_block)
    onehot = (chosen[:, None] == jnp.arange(experts, dtype=jnp.int32)[None, :]).astype(jnp.int32)
    position = jnp.sum((jnp.cumsum(onehot, axis=0) - onehot) * onehot, axis=1)
    slot_of = chosen * capacity + position
    placing = slot_of[:, None] == jnp.arange(slots, dtype=jnp.int32)[None, :]
    tok_place = jnp.any(placing.reshape(tok_rows, top_count, slots), axis=1).astype(jnp.bfloat16)
    send_grad = (
        contract_product(tok_place, grad_out, 0, 0)
        .astype(jnp.bfloat16)
        .reshape(experts, capacity, grad_out.shape[1])
    )
    send_gate = jnp.sum(jnp.where(placing, gates.reshape(per_block)[:, None], 0.0), axis=0).reshape(
        experts, capacity
    )
    recv_grad, recv_gate = (
        lax.all_to_all(send_grad, "expert", split_axis=0, concat_axis=0, tiled=True),
        lax.all_to_all(
            send_gate.astype(jnp.bfloat16), "expert", split_axis=0, concat_axis=0, tiled=True
        ).astype(send_gate.dtype),
    )
    grad_rows = recv_grad.reshape(slots, grad_out.shape[1])
    gate_rows = recv_gate.reshape(slots)
    hidden_slot_rows = hidden[0, 0]
    adapter_down_factor = adapter_a[0]
    factor_b = adapter_b[0]
    gate_scaled_rows = (gate_rows[:, None] * grad_rows.astype(jnp.float32)).astype(jnp.bfloat16)
    frozen_gradient_term = contract_product(
        grad_rows, lax.all_gather(down_weight[0], "dp", axis=0, tiled=True), 1, 1
    )
    grad_hid, slot_dgate, first_factor_term, second_factor_term = expert_terms(
        frozen_gradient_term,
        grad_rows,
        gate_rows,
        hidden_slot_rows,
        adapter_down_factor,
        factor_b,
        gate_scaled_rows,
    )
    gradient_first_factor, gradient_second_factor = (
        lax.psum(first_factor_term.astype(jnp.bfloat16), "dp").astype(jnp.float32),
        lax.psum(second_factor_term.astype(jnp.bfloat16), "dp").astype(jnp.float32),
    )
    back_gate = lax.all_to_all(
        slot_dgate.reshape(experts, capacity), "expert", split_axis=0, concat_axis=0, tiled=True
    )
    grad_gates = jnp.sum(
        jnp.where(placing, back_gate.reshape(slots)[None, :], 0.0), axis=1
    ).reshape(tok_rows, top_count)
    return (
        grad_hid[None, None],
        grad_gates,
        gradient_first_factor[None],
        gradient_second_factor[None],
    )


def flip(value, bit):
    return value + bit - 2 * bit * ((value // bit) % 2)


def xor(value, mask):
    bit = 1
    while bit <= mask:
        if mask & bit:
            value = flip(value, bit)
        bit *= 2
    return value


def one_hot(shape, pick):
    rows = lax.broadcasted_iota(jnp.int32, shape, 0)
    columns = lax.broadcasted_iota(jnp.int32, shape, 1)
    return pick(rows, columns).astype(jnp.bfloat16)


def tile_of(size, most):
    tile = most
    while size % tile:
        tile //= 2
    return tile


def fused_kernel(
    experts,
    routes_ref,
    gates_ref,
    grad_ref,
    hidden_ref,
    weight_hbm,
    a_ref,
    b_ref,
    grad_hid_ref,
    grad_gates_ref,
    grad_a_ref,
    grad_b_ref,
    tokens,
    weight,
    rows,
    before,
    back_out,
    back_in,
    weight_sem,
    send_sem,
    recv_sem,
    back_send_sem,
    back_recv_sem,
):
    me = lax.axis_index("expert")
    top_count, tok_rows = routes_ref.shape
    features = grad_ref.shape[1]
    slots, units = hidden_ref.shape
    capacity = slots // experts
    total = experts * tok_rows
    planes = experts // 4
    z, x, core = me // 4, (me // 2) % 2, me % 2
    bf16, f32 = jnp.bfloat16, jnp.float32

    load_weight = pltpu.make_async_copy(weight_hbm, weight, weight_sem)
    load_weight.start()

    barrier = pltpu.get_barrier_semaphore()
    for step in range(1, experts):
        pl.semaphore_signal(
            barrier,
            inc=1,
            device_id={"expert": lax.rem(me + step, experts)},
            device_id_type=MESH,
        )

    def place_of(plane, column, lane):
        return (column * 2 + lane) * planes + plane

    own = place_of(z, x, core)
    tokens[own, :, :features] = grad_ref[...]
    high = gates_ref[...].astype(bf16)
    low = (gates_ref[...] - high.astype(f32)).astype(bf16)
    meta = jnp.zeros((tok_rows, 128), f32)
    for part, values in enumerate((routes_ref[...].astype(f32).astype(bf16), high, low)):
        spread = one_hot((top_count, 128), lambda r, c: c == r + part * top_count)
        meta = meta + contract_product(values, spread, 0, 0)
    tokens[own, :, features:] = meta.astype(bf16)
    pl.semaphore_wait(barrier, experts - 1)

    def source_of(token):
        stored = lax.div(token, tok_rows)
        return lax.rem(stored, planes) * 4 + lax.div(stored, planes)

    def index(plane, column, lane):
        return plane * 4 + column * 2 + lane

    x_mate, core_mate = index(z, 1 - x, core), index(z, x, 1 - core)
    sent = []

    def held(first, count):
        return tokens.at[pl.ds(first, count)]

    def send(first, count, target):
        copy = pltpu.make_async_remote_copy(
            src_ref=held(first, count),
            dst_ref=held(first, count),
            send_sem=send_sem.at[len(sent)],
            recv_sem=recv_sem.at[first],
            device_id={"expert": target},
            device_id_type=MESH,
        )
        copy.start()
        sent.append(copy)

    def arrived(first, count):
        pltpu.make_async_remote_copy(
            src_ref=held(first, count),
            dst_ref=held(first, count),
            send_sem=send_sem.at[0],
            recv_sem=recv_sem.at[first],
            device_id={"expert": core_mate},
            device_id_type=MESH,
        ).wait_recv()

    near, far = 2 * (z // 2), 2 * (1 - z // 2)
    send(own, 1, x_mate)
    for step in range(1, planes):
        send(own, 1, index(xor(z, step), x, core))

    before[...] = one_hot(
        (total, total), lambda r, c: (r < c) & (lax.div(r, tok_rows) == lax.div(c, tok_rows))
    )
    low_fwd = contract_product(hidden_ref[...], a_ref[...], 1, 1)
    beside = place_of(xor(z, 1), x, core)
    arrived(beside, 1)
    send(beside, 1, x_mate)
    send(place_of(near, x, core), 2, core_mate)
    arrived(place_of(z, 1 - x, core), 1)
    for step in (2, 3):
        arrived(place_of(xor(z, step), x, core), 1)
    send(place_of(far, x, core), 2, x_mate)
    send(place_of(far, x, core), 2, core_mate)
    arrived(place_of(xor(z, 1), 1 - x, core), 1)
    send(place_of(near, 1 - x, core), 2, core_mate)
    arrived(place_of(far, 1 - x, core), 2)
    send(place_of(far, 1 - x, core), 2, core_mate)
    for column in (x, 1 - x):
        for pair in (near, far):
            arrived(place_of(pair, column, 1 - core), 2)

    gathered = tokens[:, :, features:].reshape(total, 128)
    eye = one_hot((128, 128), lambda r, c: r == c)
    turned = contract_product(eye, gathered, 1, 1)
    named = turned[:top_count] == me.astype(f32)
    gate_of = jnp.where(
        named, turned[top_count : 2 * top_count] + turned[2 * top_count : 3 * top_count], 0.0
    )
    gate_tok = jnp.sum(gate_of, axis=0, keepdims=True)
    match = jnp.sum(named.astype(f32), axis=0, keepdims=True)
    position = contract_product(
        jnp.broadcast_to(match, (8, total)).astype(bf16), before[...], 1, 0
    )[:1]
    block = source_of(lax.broadcasted_iota(jnp.int32, (1, total), 1))
    slot_of = jnp.where(match > 0.0, block.astype(f32) * capacity + position, -1.0)
    slot_ids = lax.broadcasted_iota(jnp.int32, (slots, total), 0).astype(f32)
    placing = slot_ids == slot_of
    gate = jnp.sum(jnp.where(placing, gate_tok, 0.0), axis=1, keepdims=True)
    place = placing.astype(bf16)

    wide = tile_of(features, 512)
    for start in range(0, features, wide):
        columns = slice(start, start + wide)
        rows[:, columns] = contract_product(
            place, tokens[:, :, columns].reshape(total, wide), 1, 0
        ).astype(bf16)
    low_back = contract_product(rows[...], b_ref[...], 1, 1)
    low_back_b = low_back.astype(bf16)
    load_weight.wait()
    deep = tile_of(units, 256)
    dgate = jnp.zeros((slots, 1), f32)
    for start in range(0, units, deep):
        span = slice(start, start + deep)
        through = contract_product(rows[...], weight[span, :], 1, 1)
        through = through + contract_product(low_back_b, a_ref[:, span], 1, 0)
        grad_hid_ref[:, span] = (gate * through).astype(bf16)
        dgate = dgate + jnp.sum(hidden_ref[:, span].astype(f32) * through, axis=1, keepdims=True)

    dgate_tok = jnp.sum(jnp.where(placing, dgate, 0.0), axis=0, keepdims=True)
    exact = lax.Precision.HIGHEST
    source = lax.broadcasted_iota(jnp.int32, (experts, total), 0)
    owner = source_of(lax.broadcasted_iota(jnp.int32, (experts, total), 1))
    by_source = lax.dot_general(
        jnp.where(source == owner, dgate_tok, 0.0),
        one_hot((total, 128), lambda r, c: lax.rem(r, tok_rows) == c).astype(f32),
        (((1,), (0,)), ((), ())),
        precision=exact,
        preferred_element_type=f32,
    )
    back_out[...] = jnp.broadcast_to(by_source[:, None, :], back_out.shape)
    returned = []
    for step in range(1, experts):
        target = lax.rem(me + step, experts)
        copy = pltpu.make_async_remote_copy(
            src_ref=back_out.at[target],
            dst_ref=back_in.at[me],
            send_sem=back_send_sem.at[step],
            recv_sem=back_recv_sem.at[me],
            device_id={"expert": target},
            device_id_type=MESH,
        )
        copy.start()
        returned.append(copy)
    back_in[me] = back_out[me]

    weighted = (gate * low_back).astype(bf16)
    grad_a_ref[...] = contract_product(weighted, hidden_ref[...], 0, 0)
    scaled = (gate * low_fwd).astype(bf16)
    for start in range(0, features, wide):
        columns = slice(start, start + wide)
        grad_b_ref[:, columns] = contract_product(scaled, rows[:, columns], 0, 0)

    for copy in sent:
        copy.wait_send()
    for copy in returned:
        copy.wait_send()
    for step in range(1, experts):
        origin = lax.rem(me + step, experts)
        pltpu.make_async_remote_copy(
            src_ref=back_out.at[origin],
            dst_ref=back_in.at[origin],
            send_sem=back_send_sem.at[step],
            recv_sem=back_recv_sem.at[origin],
            device_id={"expert": origin},
            device_id_type=MESH,
        ).wait_recv()
    back = lax.dot_general(
        back_in[:, 0, :],
        one_hot((128, tok_rows), lambda r, c: r == c).astype(f32),
        (((1,), (0,)), ((), ())),
        precision=exact,
        preferred_element_type=f32,
    )
    chosen = routes_ref[...]
    picked = jnp.zeros((top_count, tok_rows), f32)
    for expert in range(experts):
        picked = picked + jnp.where(chosen == expert, back[expert : expert + 1, :], 0.0)
    grad_gates_ref[...] = picked


def copy_kernel(*refs):
    count = len(refs) // 2
    for i in range(count):
        refs[count + i][...] = refs[i][...]


def fused_shards(experts, routes, gates, grad_out, hidden, down_weight, adapter_a, adapter_b):
    tok_rows, top_count = routes.shape
    features = grad_out.shape[1]
    slots, units = hidden.shape[2:]
    vmem = pl.BlockSpec(memory_space=pltpu.VMEM)
    hbm = pl.BlockSpec(memory_space=pl.ANY)
    dma = pltpu.SemaphoreType.DMA
    out_shape = (
        jax.ShapeDtypeStruct((slots, units), jnp.bfloat16),
        jax.ShapeDtypeStruct((top_count, tok_rows), jnp.float32),
        jax.ShapeDtypeStruct(adapter_a.shape[1:], jnp.float32),
        jax.ShapeDtypeStruct(adapter_b.shape[1:], jnp.float32),
    )
    results = pl.pallas_call(
        functools.partial(fused_kernel, experts),
        out_shape=out_shape,
        in_specs=[vmem] * 4 + [hbm] + [vmem] * 2,
        out_specs=(vmem,) * 4,
        scratch_shapes=[
            pltpu.VMEM((experts, tok_rows, features + 128), jnp.bfloat16),
            pltpu.VMEM((units, features), jnp.bfloat16),
            pltpu.VMEM((slots, features), jnp.bfloat16),
            pltpu.VMEM((experts * tok_rows, experts * tok_rows), jnp.bfloat16),
            pltpu.VMEM((experts, 8, 128), jnp.float32),
            pltpu.VMEM((experts, 8, 128), jnp.float32),
            dma,
            dma((experts,)),
            dma((experts,)),
            dma((experts,)),
            dma((experts,)),
        ],
        compiler_params=pltpu.CompilerParams(
            collective_id=0, has_side_effects=True, vmem_limit_bytes=56 * 1024 * 1024
        ),
    )(routes.T, gates.T, grad_out, hidden[0, 0], down_weight[0], adapter_a[0], adapter_b[0])
    grad_hid, grad_gates, grad_a, grad_b = pl.pallas_call(
        copy_kernel,
        out_shape=out_shape,
        in_specs=[vmem] * 4,
        out_specs=(vmem,) * 4,
        compiler_params=pltpu.CompilerParams(vmem_limit_bytes=60 * 1024 * 1024),
    )(*results)
    return grad_hid[None, None], grad_gates.T, grad_a[None], grad_b[None]


def solution(mesh):
    placed = (
        P(("job", "dp", "expert"), None),
        P(("job", "dp", "expert"), None),
        P(("job", "dp", "expert"), None),
        P("expert", ("job", "dp"), None, None),
        P("expert", "dp", None),
        P(("job", "expert"), None, None),
        P(("job", "expert"), None, None),
    )
    experts = mesh.shape["expert"]
    fused = mesh.shape["dp"] == 1 and experts == 16
    return jax.shard_map(
        functools.partial(fused_shards, experts) if fused else shards,
        mesh=mesh,
        in_specs=placed,
        out_specs=(
            P("expert", ("job", "dp"), None, None),
            P(("job", "dp", "expert"), None),
            P(("job", "expert"), None, None),
            P(("job", "expert"), None, None),
        ),
        check_vma=False,
    )
```

```python
import functools

import jax
import jax.numpy as jnp
from jax import lax
from jax.experimental import pallas as pl
from jax.experimental.pallas import tpu as pltpu
from jax.sharding import PartitionSpec as P

ADAPTER_SCALING = 1.0
MESH = pl.DeviceIdType.MESH


def contract_product(left, right, left_dim, right_dim):
    return lax.dot_general(
        left, right, (((left_dim,), (right_dim,)), ((), ())), preferred_element_type=jnp.float32
    )


def expert_terms(
    frozen_gradient_term,
    grad_rows,
    gate_rows,
    hidden_slot_rows,
    adapter_down_factor,
    factor_b,
    gate_scaled_rows,
):
    lowrank_backward = contract_product(grad_rows, factor_b, 1, 1)
    passed_gradient = frozen_gradient_term + ADAPTER_SCALING * jnp.dot(
        lowrank_backward.astype(jnp.bfloat16),
        adapter_down_factor,
        preferred_element_type=jnp.float32,
    )
    grad_hid = (gate_rows[:, None] * passed_gradient).astype(jnp.bfloat16)
    slot_dgate = jnp.sum(hidden_slot_rows.astype(jnp.float32) * passed_gradient, axis=1)
    gate_weighted_output = (gate_rows[:, None] * lowrank_backward).astype(jnp.bfloat16)
    first_factor_term = ADAPTER_SCALING * contract_product(
        gate_weighted_output, hidden_slot_rows, 0, 0
    )
    lowrank_forward = contract_product(hidden_slot_rows, adapter_down_factor, 1, 1).astype(
        jnp.bfloat16
    )
    second_factor_term = ADAPTER_SCALING * contract_product(lowrank_forward, gate_scaled_rows, 0, 0)
    return (grad_hid, slot_dgate, first_factor_term, second_factor_term)


def shards(routes, gates, grad_out, hidden, down_weight, adapter_a, adapter_b):
    tok_rows, top_count = routes.shape
    experts = lax.axis_size("expert")
    slots = hidden.shape[2]
    capacity = slots // experts
    per_block = tok_rows * top_count
    chosen = routes.reshape(per_block)
    onehot = (chosen[:, None] == jnp.arange(experts, dtype=jnp.int32)[None, :]).astype(jnp.int32)
    position = jnp.sum((jnp.cumsum(onehot, axis=0) - onehot) * onehot, axis=1)
    slot_of = chosen * capacity + position
    placing = slot_of[:, None] == jnp.arange(slots, dtype=jnp.int32)[None, :]
    tok_place = jnp.any(placing.reshape(tok_rows, top_count, slots), axis=1).astype(jnp.bfloat16)
    send_grad = (
        contract_product(tok_place, grad_out, 0, 0)
        .astype(jnp.bfloat16)
        .reshape(experts, capacity, grad_out.shape[1])
    )
    send_gate = jnp.sum(jnp.where(placing, gates.reshape(per_block)[:, None], 0.0), axis=0).reshape(
        experts, capacity
    )
    recv_grad, recv_gate = (
        lax.all_to_all(send_grad, "expert", split_axis=0, concat_axis=0, tiled=True),
        lax.all_to_all(
            send_gate.astype(jnp.bfloat16), "expert", split_axis=0, concat_axis=0, tiled=True
        ).astype(send_gate.dtype),
    )
    grad_rows = recv_grad.reshape(slots, grad_out.shape[1])
    gate_rows = recv_gate.reshape(slots)
    hidden_slot_rows = hidden[0, 0]
    adapter_down_factor = adapter_a[0]
    factor_b = adapter_b[0]
    gate_scaled_rows = (gate_rows[:, None] * grad_rows.astype(jnp.float32)).astype(jnp.bfloat16)
    frozen_gradient_term = contract_product(
        grad_rows, lax.all_gather(down_weight[0], "dp", axis=0, tiled=True), 1, 1
    )
    grad_hid, slot_dgate, first_factor_term, second_factor_term = expert_terms(
        frozen_gradient_term,
        grad_rows,
        gate_rows,
        hidden_slot_rows,
        adapter_down_factor,
        factor_b,
        gate_scaled_rows,
    )
    gradient_first_factor, gradient_second_factor = (
        lax.psum(first_factor_term.astype(jnp.bfloat16), "dp").astype(jnp.float32),
        lax.psum(second_factor_term.astype(jnp.bfloat16), "dp").astype(jnp.float32),
    )
    back_gate = lax.all_to_all(
        slot_dgate.reshape(experts, capacity), "expert", split_axis=0, concat_axis=0, tiled=True
    )
    grad_gates = jnp.sum(
        jnp.where(placing, back_gate.reshape(slots)[None, :], 0.0), axis=1
    ).reshape(tok_rows, top_count)
    return (
        grad_hid[None, None],
        grad_gates,
        gradient_first_factor[None],
        gradient_second_factor[None],
    )


def flip(value, bit):
    return value + bit - 2 * bit * ((value // bit) % 2)


def xor(value, mask):
    bit = 1
    while bit <= mask:
        if mask & bit:
            value = flip(value, bit)
        bit *= 2
    return value


def one_hot(shape, pick):
    rows = lax.broadcasted_iota(jnp.int32, shape, 0)
    columns = lax.broadcasted_iota(jnp.int32, shape, 1)
    return pick(rows, columns).astype(jnp.bfloat16)


def tile_of(size, most):
    tile = most
    while size % tile:
        tile //= 2
    return tile


def fused_kernel(
    experts,
    routes_ref,
    gates_ref,
    grad_ref,
    hidden_ref,
    weight_hbm,
    a_ref,
    b_ref,
    grad_hid_ref,
    grad_gates_ref,
    grad_a_ref,
    grad_b_ref,
    tokens,
    weight,
    rows,
    before,
    back_out,
    back_in,
    weight_sem,
    send_sem,
    recv_sem,
    back_send_sem,
    back_recv_sem,
):
    me = lax.axis_index("expert")
    top_count, tok_rows = routes_ref.shape
    features = grad_ref.shape[1]
    slots, units = hidden_ref.shape
    capacity = slots // experts
    total = experts * tok_rows
    planes = experts // 4
    z, x, core = me // 4, (me // 2) % 2, me % 2
    bf16, f32 = jnp.bfloat16, jnp.float32

    load_weight = pltpu.make_async_copy(weight_hbm, weight, weight_sem)
    load_weight.start()

    barrier = pltpu.get_barrier_semaphore()
    for step in range(1, experts):
        pl.semaphore_signal(
            barrier,
            inc=1,
            device_id={"expert": lax.rem(me + step, experts)},
            device_id_type=MESH,
        )

    def place_of(plane, column, lane):
        return (column * 2 + lane) * planes + plane

    own = place_of(z, x, core)
    tokens[own, :, :features] = grad_ref[...]
    high = gates_ref[...].astype(bf16)
    low = (gates_ref[...] - high.astype(f32)).astype(bf16)
    meta = jnp.zeros((tok_rows, 128), f32)
    for part, values in enumerate((routes_ref[...].astype(f32).astype(bf16), high, low)):
        spread = one_hot((top_count, 128), lambda r, c: c == r + part * top_count)
        meta = meta + contract_product(values, spread, 0, 0)
    tokens[own, :, features:] = meta.astype(bf16)
    pl.semaphore_wait(barrier, experts - 1)

    def source_of(token):
        stored = lax.div(token, tok_rows)
        return lax.rem(stored, planes) * 4 + lax.div(stored, planes)

    def index(plane, column, lane):
        return plane * 4 + column * 2 + lane

    x_mate, core_mate = index(z, 1 - x, core), index(z, x, 1 - core)
    sent = []

    def held(first, count):
        return tokens.at[pl.ds(first, count)]

    def send(first, count, target):
        copy = pltpu.make_async_remote_copy(
            src_ref=held(first, count),
            dst_ref=held(first, count),
            send_sem=send_sem.at[len(sent)],
            recv_sem=recv_sem.at[first],
            device_id={"expert": target},
            device_id_type=MESH,
        )
        copy.start()
        sent.append(copy)

    def arrived(first, count):
        pltpu.make_async_remote_copy(
            src_ref=held(first, count),
            dst_ref=held(first, count),
            send_sem=send_sem.at[0],
            recv_sem=recv_sem.at[first],
            device_id={"expert": core_mate},
            device_id_type=MESH,
        ).wait_recv()

    near, far = 2 * (z // 2), 2 * (1 - z // 2)
    send(own, 1, x_mate)
    for step in range(1, planes):
        send(own, 1, index(xor(z, step), x, core))

    before[...] = one_hot(
        (total, total), lambda r, c: (r < c) & (lax.div(r, tok_rows) == lax.div(c, tok_rows))
    )
    low_fwd = contract_product(hidden_ref[...], a_ref[...], 1, 1)
    beside = place_of(xor(z, 1), x, core)
    arrived(beside, 1)
    send(beside, 1, x_mate)
    send(place_of(near, x, core), 2, core_mate)
    arrived(place_of(z, 1 - x, core), 1)
    for step in (2, 3):
        distant = place_of(xor(z, step), x, core)
        arrived(distant, 1)
        send(distant, 1, x_mate)
    send(place_of(far, x, core), 2, core_mate)
    arrived(place_of(xor(z, 1), 1 - x, core), 1)
    send(place_of(near, 1 - x, core), 2, core_mate)
    for step in (2, 3):
        arrived(place_of(xor(z, step), 1 - x, core), 1)
    send(place_of(far, 1 - x, core), 2, core_mate)
    for column in (x, 1 - x):
        for pair in (near, far):
            arrived(place_of(pair, column, 1 - core), 2)

    gathered = tokens[:, :, features:].reshape(total, 128)
    eye = one_hot((128, 128), lambda r, c: r == c)
    turned = contract_product(eye, gathered, 1, 1)
    named = turned[:top_count] == me.astype(f32)
    gate_of = jnp.where(
        named, turned[top_count : 2 * top_count] + turned[2 * top_count : 3 * top_count], 0.0
    )
    gate_tok = jnp.sum(gate_of, axis=0, keepdims=True)
    match = jnp.sum(named.astype(f32), axis=0, keepdims=True)
    position = contract_product(
        jnp.broadcast_to(match, (8, total)).astype(bf16), before[...], 1, 0
    )[:1]
    block = source_of(lax.broadcasted_iota(jnp.int32, (1, total), 1))
    slot_of = jnp.where(match > 0.0, block.astype(f32) * capacity + position, -1.0)
    slot_ids = lax.broadcasted_iota(jnp.int32, (slots, total), 0).astype(f32)
    placing = slot_ids == slot_of
    gate = jnp.sum(jnp.where(placing, gate_tok, 0.0), axis=1, keepdims=True)
    place = placing.astype(bf16)

    wide = tile_of(features, 512)
    for start in range(0, features, wide):
        columns = slice(start, start + wide)
        rows[:, columns] = contract_product(
            place, tokens[:, :, columns].reshape(total, wide), 1, 0
        ).astype(bf16)
    low_back = contract_product(rows[...], b_ref[...], 1, 1)
    low_back_b = low_back.astype(bf16)
    load_weight.wait()
    deep = tile_of(units, 256)
    dgate = jnp.zeros((slots, 1), f32)
    for start in range(0, units, deep):
        span = slice(start, start + deep)
        through = contract_product(rows[...], weight[span, :], 1, 1)
        through = through + contract_product(low_back_b, a_ref[:, span], 1, 0)
        grad_hid_ref[:, span] = (gate * through).astype(bf16)
        dgate = dgate + jnp.sum(hidden_ref[:, span].astype(f32) * through, axis=1, keepdims=True)

    dgate_tok = jnp.sum(jnp.where(placing, dgate, 0.0), axis=0, keepdims=True)
    exact = lax.Precision.HIGHEST
    source = lax.broadcasted_iota(jnp.int32, (experts, total), 0)
    owner = source_of(lax.broadcasted_iota(jnp.int32, (experts, total), 1))
    by_source = lax.dot_general(
        jnp.where(source == owner, dgate_tok, 0.0),
        one_hot((total, 128), lambda r, c: lax.rem(r, tok_rows) == c).astype(f32),
        (((1,), (0,)), ((), ())),
        precision=exact,
        preferred_element_type=f32,
    )
    back_out[...] = jnp.broadcast_to(by_source[:, None, :], back_out.shape)
    returned = []
    for step in range(1, experts):
        target = lax.rem(me + step, experts)
        copy = pltpu.make_async_remote_copy(
            src_ref=back_out.at[target],
            dst_ref=back_in.at[me],
            send_sem=back_send_sem.at[step],
            recv_sem=back_recv_sem.at[me],
            device_id={"expert": target},
            device_id_type=MESH,
        )
        copy.start()
        returned.append(copy)
    back_in[me] = back_out[me]

    weighted = (gate * low_back).astype(bf16)
    grad_a_ref[...] = contract_product(weighted, hidden_ref[...], 0, 0)
    scaled = (gate * low_fwd).astype(bf16)
    for start in range(0, features, wide):
        columns = slice(start, start + wide)
        grad_b_ref[:, columns] = contract_product(scaled, rows[:, columns], 0, 0)

    for copy in sent:
        copy.wait_send()
    for copy in returned:
        copy.wait_send()
    for step in range(1, experts):
        origin = lax.rem(me + step, experts)
        pltpu.make_async_remote_copy(
            src_ref=back_out.at[origin],
            dst_ref=back_in.at[origin],
            send_sem=back_send_sem.at[step],
            recv_sem=back_recv_sem.at[origin],
            device_id={"expert": origin},
            device_id_type=MESH,
        ).wait_recv()
    back = lax.dot_general(
        back_in[:, 0, :],
        one_hot((128, tok_rows), lambda r, c: r == c).astype(f32),
        (((1,), (0,)), ((), ())),
        precision=exact,
        preferred_element_type=f32,
    )
    chosen = routes_ref[...]
    picked = jnp.zeros((top_count, tok_rows), f32)
    for expert in range(experts):
        picked = picked + jnp.where(chosen == expert, back[expert : expert + 1, :], 0.0)
    grad_gates_ref[...] = picked


def copy_kernel(*refs):
    count = len(refs) // 2
    for i in range(count):
        refs[count + i][...] = refs[i][...]


def fused_shards(experts, routes, gates, grad_out, hidden, down_weight, adapter_a, adapter_b):
    tok_rows, top_count = routes.shape
    features = grad_out.shape[1]
    slots, units = hidden.shape[2:]
    vmem = pl.BlockSpec(memory_space=pltpu.VMEM)
    hbm = pl.BlockSpec(memory_space=pl.ANY)
    dma = pltpu.SemaphoreType.DMA
    out_shape = (
        jax.ShapeDtypeStruct((slots, units), jnp.bfloat16),
        jax.ShapeDtypeStruct((top_count, tok_rows), jnp.float32),
        jax.ShapeDtypeStruct(adapter_a.shape[1:], jnp.float32),
        jax.ShapeDtypeStruct(adapter_b.shape[1:], jnp.float32),
    )
    results = pl.pallas_call(
        functools.partial(fused_kernel, experts),
        out_shape=out_shape,
        in_specs=[vmem] * 4 + [hbm] + [vmem] * 2,
        out_specs=(vmem,) * 4,
        scratch_shapes=[
            pltpu.VMEM((experts, tok_rows, features + 128), jnp.bfloat16),
            pltpu.VMEM((units, features), jnp.bfloat16),
            pltpu.VMEM((slots, features), jnp.bfloat16),
            pltpu.VMEM((experts * tok_rows, experts * tok_rows), jnp.bfloat16),
            pltpu.VMEM((experts, 8, 128), jnp.float32),
            pltpu.VMEM((experts, 8, 128), jnp.float32),
            dma,
            dma((experts,)),
            dma((experts,)),
            dma((experts,)),
            dma((experts,)),
        ],
        compiler_params=pltpu.CompilerParams(
            collective_id=0, has_side_effects=True, vmem_limit_bytes=56 * 1024 * 1024
        ),
    )(routes.T, gates.T, grad_out, hidden[0, 0], down_weight[0], adapter_a[0], adapter_b[0])
    grad_hid, grad_gates, grad_a, grad_b = pl.pallas_call(
        copy_kernel,
        out_shape=out_shape,
        in_specs=[vmem] * 4,
        out_specs=(vmem,) * 4,
        compiler_params=pltpu.CompilerParams(vmem_limit_bytes=60 * 1024 * 1024),
    )(*results)
    return grad_hid[None, None], grad_gates.T, grad_a[None], grad_b[None]


def solution(mesh):
    placed = (
        P(("job", "dp", "expert"), None),
        P(("job", "dp", "expert"), None),
        P(("job", "dp", "expert"), None),
        P("expert", ("job", "dp"), None, None),
        P("expert", "dp", None),
        P(("job", "expert"), None, None),
        P(("job", "expert"), None, None),
    )
    experts = mesh.shape["expert"]
    fused = mesh.shape["dp"] == 1 and experts == 16
    return jax.shard_map(
        functools.partial(fused_shards, experts) if fused else shards,
        mesh=mesh,
        in_specs=placed,
        out_specs=(
            P("expert", ("job", "dp"), None, None),
            P(("job", "dp", "expert"), None),
            P(("job", "expert"), None, None),
            P(("job", "expert"), None, None),
        ),
        check_vma=False,
    )
```

```python
import functools

import jax
import jax.numpy as jnp
from jax import lax
from jax.experimental import pallas as pl
from jax.experimental.pallas import tpu as pltpu
from jax.sharding import PartitionSpec as P

ADAPTER_SCALING = 1.0
MESH = pl.DeviceIdType.MESH


def contract_product(left, right, left_dim, right_dim):
    return lax.dot_general(
        left, right, (((left_dim,), (right_dim,)), ((), ())), preferred_element_type=jnp.float32
    )


def expert_terms(
    frozen_gradient_term,
    grad_rows,
    gate_rows,
    hidden_slot_rows,
    adapter_down_factor,
    factor_b,
    gate_scaled_rows,
):
    lowrank_backward = contract_product(grad_rows, factor_b, 1, 1)
    passed_gradient = frozen_gradient_term + ADAPTER_SCALING * jnp.dot(
        lowrank_backward.astype(jnp.bfloat16),
        adapter_down_factor,
        preferred_element_type=jnp.float32,
    )
    grad_hid = (gate_rows[:, None] * passed_gradient).astype(jnp.bfloat16)
    slot_dgate = jnp.sum(hidden_slot_rows.astype(jnp.float32) * passed_gradient, axis=1)
    gate_weighted_output = (gate_rows[:, None] * lowrank_backward).astype(jnp.bfloat16)
    first_factor_term = ADAPTER_SCALING * contract_product(
        gate_weighted_output, hidden_slot_rows, 0, 0
    )
    lowrank_forward = contract_product(hidden_slot_rows, adapter_down_factor, 1, 1).astype(
        jnp.bfloat16
    )
    second_factor_term = ADAPTER_SCALING * contract_product(lowrank_forward, gate_scaled_rows, 0, 0)
    return (grad_hid, slot_dgate, first_factor_term, second_factor_term)


def shards(routes, gates, grad_out, hidden, down_weight, adapter_a, adapter_b):
    tok_rows, top_count = routes.shape
    experts = lax.axis_size("expert")
    slots = hidden.shape[2]
    capacity = slots // experts
    per_block = tok_rows * top_count
    chosen = routes.reshape(per_block)
    onehot = (chosen[:, None] == jnp.arange(experts, dtype=jnp.int32)[None, :]).astype(jnp.int32)
    position = jnp.sum((jnp.cumsum(onehot, axis=0) - onehot) * onehot, axis=1)
    slot_of = chosen * capacity + position
    placing = slot_of[:, None] == jnp.arange(slots, dtype=jnp.int32)[None, :]
    tok_place = jnp.any(placing.reshape(tok_rows, top_count, slots), axis=1).astype(jnp.bfloat16)
    send_grad = (
        contract_product(tok_place, grad_out, 0, 0)
        .astype(jnp.bfloat16)
        .reshape(experts, capacity, grad_out.shape[1])
    )
    send_gate = jnp.sum(jnp.where(placing, gates.reshape(per_block)[:, None], 0.0), axis=0).reshape(
        experts, capacity
    )
    recv_grad, recv_gate = (
        lax.all_to_all(send_grad, "expert", split_axis=0, concat_axis=0, tiled=True),
        lax.all_to_all(
            send_gate.astype(jnp.bfloat16), "expert", split_axis=0, concat_axis=0, tiled=True
        ).astype(send_gate.dtype),
    )
    grad_rows = recv_grad.reshape(slots, grad_out.shape[1])
    gate_rows = recv_gate.reshape(slots)
    hidden_slot_rows = hidden[0, 0]
    adapter_down_factor = adapter_a[0]
    factor_b = adapter_b[0]
    gate_scaled_rows = (gate_rows[:, None] * grad_rows.astype(jnp.float32)).astype(jnp.bfloat16)
    frozen_gradient_term = contract_product(
        grad_rows, lax.all_gather(down_weight[0], "dp", axis=0, tiled=True), 1, 1
    )
    grad_hid, slot_dgate, first_factor_term, second_factor_term = expert_terms(
        frozen_gradient_term,
        grad_rows,
        gate_rows,
        hidden_slot_rows,
        adapter_down_factor,
        factor_b,
        gate_scaled_rows,
    )
    gradient_first_factor, gradient_second_factor = (
        lax.psum(first_factor_term.astype(jnp.bfloat16), "dp").astype(jnp.float32),
        lax.psum(second_factor_term.astype(jnp.bfloat16), "dp").astype(jnp.float32),
    )
    back_gate = lax.all_to_all(
        slot_dgate.reshape(experts, capacity), "expert", split_axis=0, concat_axis=0, tiled=True
    )
    grad_gates = jnp.sum(
        jnp.where(placing, back_gate.reshape(slots)[None, :], 0.0), axis=1
    ).reshape(tok_rows, top_count)
    return (
        grad_hid[None, None],
        grad_gates,
        gradient_first_factor[None],
        gradient_second_factor[None],
    )


def flip(value, bit):
    return value + bit - 2 * bit * ((value // bit) % 2)


def xor(value, mask):
    bit = 1
    while bit <= mask:
        if mask & bit:
            value = flip(value, bit)
        bit *= 2
    return value


def one_hot(shape, pick):
    rows = lax.broadcasted_iota(jnp.int32, shape, 0)
    columns = lax.broadcasted_iota(jnp.int32, shape, 1)
    return pick(rows, columns).astype(jnp.bfloat16)


def tile_of(size, most):
    tile = most
    while size % tile:
        tile //= 2
    return tile


def fused_kernel(
    experts,
    routes_ref,
    gates_ref,
    grad_ref,
    hidden_ref,
    weight_hbm,
    a_ref,
    b_ref,
    grad_hid_ref,
    grad_gates_ref,
    grad_a_ref,
    grad_b_ref,
    tokens,
    weight,
    rows,
    before,
    back_out,
    back_in,
    weight_sem,
    send_sem,
    recv_sem,
    back_send_sem,
    back_recv_sem,
):
    me = lax.axis_index("expert")
    top_count, tok_rows = routes_ref.shape
    features = grad_ref.shape[1]
    slots, units = hidden_ref.shape
    capacity = slots // experts
    total = experts * tok_rows
    planes = experts // 4
    z, x, core = me // 4, (me // 2) % 2, me % 2
    bf16, f32 = jnp.bfloat16, jnp.float32

    load_weight = pltpu.make_async_copy(weight_hbm, weight, weight_sem)
    load_weight.start()

    barrier = pltpu.get_barrier_semaphore()
    for step in range(1, experts):
        pl.semaphore_signal(
            barrier,
            inc=1,
            device_id={"expert": lax.rem(me + step, experts)},
            device_id_type=MESH,
        )

    def place_of(plane, column, lane):
        return (column * 2 + lane) * planes + plane

    own = place_of(z, x, core)
    tokens[own, :, :features] = grad_ref[...]
    high = gates_ref[...].astype(bf16)
    low = (gates_ref[...] - high.astype(f32)).astype(bf16)
    meta = jnp.zeros((tok_rows, 128), f32)
    for part, values in enumerate((routes_ref[...].astype(f32).astype(bf16), high, low)):
        spread = one_hot((top_count, 128), lambda r, c: c == r + part * top_count)
        meta = meta + contract_product(values, spread, 0, 0)
    tokens[own, :, features:] = meta.astype(bf16)
    pl.semaphore_wait(barrier, experts - 1)

    def source_of(token):
        stored = lax.div(token, tok_rows)
        return lax.rem(stored, planes) * 4 + lax.div(stored, planes)

    def index(plane, column, lane):
        return plane * 4 + column * 2 + lane

    x_mate, core_mate = index(z, 1 - x, core), index(z, x, 1 - core)
    sent = []

    def held(first, count):
        return tokens.at[pl.ds(first, count)]

    def send(first, count, target):
        copy = pltpu.make_async_remote_copy(
            src_ref=held(first, count),
            dst_ref=held(first, count),
            send_sem=send_sem.at[len(sent)],
            recv_sem=recv_sem.at[first],
            device_id={"expert": target},
            device_id_type=MESH,
        )
        copy.start()
        sent.append(copy)

    def arrived(first, count):
        pltpu.make_async_remote_copy(
            src_ref=held(first, count),
            dst_ref=held(first, count),
            send_sem=send_sem.at[0],
            recv_sem=recv_sem.at[first],
            device_id={"expert": core_mate},
            device_id_type=MESH,
        ).wait_recv()

    near, far = 2 * (z // 2), 2 * (1 - z // 2)
    inner = (z + 1) // 2 == 1
    z_mate, middle_mate = index(xor(z, 1), x, core), index(xor(z, 3), x, core)
    beside = place_of(xor(z, 1), x, core)
    far_inner, far_outer = 2 - z // 2, 3 * (1 - z // 2)
    hops = [
        (own, middle_mate),
        (beside, middle_mate),
        (place_of(far_inner, x, core), z_mate),
        (place_of(far_outer, x, core), z_mate),
    ]

    def hop(number):
        shard, target = hops[number]
        return pltpu.make_async_remote_copy(
            src_ref=held(shard, 1),
            dst_ref=held(shard, 1),
            send_sem=send_sem.at[experts - 1 - number],
            recv_sem=recv_sem.at[shard],
            device_id={"expert": target},
            device_id_type=MESH,
        )

    def pass_on(number):
        @pl.when(inner)
        def _():
            hop(number).start()

    send(own, 1, z_mate)
    pass_on(0)
    send(own, 1, x_mate)

    before[...] = one_hot(
        (total, total), lambda r, c: (r < c) & (lax.div(r, tok_rows) == lax.div(c, tok_rows))
    )
    low_fwd = contract_product(hidden_ref[...], a_ref[...], 1, 1)
    arrived(beside, 1)
    pass_on(1)
    send(beside, 1, x_mate)
    send(place_of(near, x, core), 2, core_mate)
    for number, plane in ((2, far_inner), (3, far_outer)):
        distant = place_of(plane, x, core)
        arrived(distant, 1)
        pass_on(number)
        send(distant, 1, x_mate)
    send(place_of(far, x, core), 2, core_mate)
    arrived(place_of(z, 1 - x, core), 1)
    arrived(place_of(xor(z, 1), 1 - x, core), 1)
    send(place_of(near, 1 - x, core), 2, core_mate)
    for step in (2, 3):
        arrived(place_of(xor(z, step), 1 - x, core), 1)
    send(place_of(far, 1 - x, core), 2, core_mate)
    for column in (x, 1 - x):
        for pair in (near, far):
            arrived(place_of(pair, column, 1 - core), 2)

    gathered = tokens[:, :, features:].reshape(total, 128)
    eye = one_hot((128, 128), lambda r, c: r == c)
    turned = contract_product(eye, gathered, 1, 1)
    named = turned[:top_count] == me.astype(f32)
    gate_of = jnp.where(
        named, turned[top_count : 2 * top_count] + turned[2 * top_count : 3 * top_count], 0.0
    )
    gate_tok = jnp.sum(gate_of, axis=0, keepdims=True)
    match = jnp.sum(named.astype(f32), axis=0, keepdims=True)
    position = contract_product(
        jnp.broadcast_to(match, (8, total)).astype(bf16), before[...], 1, 0
    )[:1]
    block = source_of(lax.broadcasted_iota(jnp.int32, (1, total), 1))
    slot_of = jnp.where(match > 0.0, block.astype(f32) * capacity + position, -1.0)
    slot_ids = lax.broadcasted_iota(jnp.int32, (slots, total), 0).astype(f32)
    placing = slot_ids == slot_of
    gate = jnp.sum(jnp.where(placing, gate_tok, 0.0), axis=1, keepdims=True)
    place = placing.astype(bf16)

    wide = tile_of(features, 512)
    for start in range(0, features, wide):
        columns = slice(start, start + wide)
        rows[:, columns] = contract_product(
            place, tokens[:, :, columns].reshape(total, wide), 1, 0
        ).astype(bf16)
    low_back = contract_product(rows[...], b_ref[...], 1, 1)
    low_back_b = low_back.astype(bf16)
    load_weight.wait()
    deep = tile_of(units, 256)
    dgate = jnp.zeros((slots, 1), f32)
    for start in range(0, units, deep):
        span = slice(start, start + deep)
        through = contract_product(rows[...], weight[span, :], 1, 1)
        through = through + contract_product(low_back_b, a_ref[:, span], 1, 0)
        grad_hid_ref[:, span] = (gate * through).astype(bf16)
        dgate = dgate + jnp.sum(hidden_ref[:, span].astype(f32) * through, axis=1, keepdims=True)

    dgate_tok = jnp.sum(jnp.where(placing, dgate, 0.0), axis=0, keepdims=True)
    exact = lax.Precision.HIGHEST
    source = lax.broadcasted_iota(jnp.int32, (experts, total), 0)
    owner = source_of(lax.broadcasted_iota(jnp.int32, (experts, total), 1))
    by_source = lax.dot_general(
        jnp.where(source == owner, dgate_tok, 0.0),
        one_hot((total, 128), lambda r, c: lax.rem(r, tok_rows) == c).astype(f32),
        (((1,), (0,)), ((), ())),
        precision=exact,
        preferred_element_type=f32,
    )
    back_out[...] = jnp.broadcast_to(by_source[:, None, :], back_out.shape)
    returned = []
    for step in range(1, experts):
        target = lax.rem(me + step, experts)
        copy = pltpu.make_async_remote_copy(
            src_ref=back_out.at[target],
            dst_ref=back_in.at[me],
            send_sem=back_send_sem.at[step],
            recv_sem=back_recv_sem.at[me],
            device_id={"expert": target},
            device_id_type=MESH,
        )
        copy.start()
        returned.append(copy)
    back_in[me] = back_out[me]

    weighted = (gate * low_back).astype(bf16)
    grad_a_ref[...] = contract_product(weighted, hidden_ref[...], 0, 0)
    scaled = (gate * low_fwd).astype(bf16)
    for start in range(0, features, wide):
        columns = slice(start, start + wide)
        grad_b_ref[:, columns] = contract_product(scaled, rows[:, columns], 0, 0)

    for copy in sent:
        copy.wait_send()

    @pl.when(inner)
    def _():
        for number in range(len(hops)):
            hop(number).wait_send()

    for copy in returned:
        copy.wait_send()
    for step in range(1, experts):
        origin = lax.rem(me + step, experts)
        pltpu.make_async_remote_copy(
            src_ref=back_out.at[origin],
            dst_ref=back_in.at[origin],
            send_sem=back_send_sem.at[step],
            recv_sem=back_recv_sem.at[origin],
            device_id={"expert": origin},
            device_id_type=MESH,
        ).wait_recv()
    back = lax.dot_general(
        back_in[:, 0, :],
        one_hot((128, tok_rows), lambda r, c: r == c).astype(f32),
        (((1,), (0,)), ((), ())),
        precision=exact,
        preferred_element_type=f32,
    )
    chosen = routes_ref[...]
    picked = jnp.zeros((top_count, tok_rows), f32)
    for expert in range(experts):
        picked = picked + jnp.where(chosen == expert, back[expert : expert + 1, :], 0.0)
    grad_gates_ref[...] = picked


def copy_kernel(*refs):
    count = len(refs) // 2
    for i in range(count):
        refs[count + i][...] = refs[i][...]


def fused_shards(experts, routes, gates, grad_out, hidden, down_weight, adapter_a, adapter_b):
    tok_rows, top_count = routes.shape
    features = grad_out.shape[1]
    slots, units = hidden.shape[2:]
    vmem = pl.BlockSpec(memory_space=pltpu.VMEM)
    hbm = pl.BlockSpec(memory_space=pl.ANY)
    dma = pltpu.SemaphoreType.DMA
    out_shape = (
        jax.ShapeDtypeStruct((slots, units), jnp.bfloat16),
        jax.ShapeDtypeStruct((top_count, tok_rows), jnp.float32),
        jax.ShapeDtypeStruct(adapter_a.shape[1:], jnp.float32),
        jax.ShapeDtypeStruct(adapter_b.shape[1:], jnp.float32),
    )
    results = pl.pallas_call(
        functools.partial(fused_kernel, experts),
        out_shape=out_shape,
        in_specs=[vmem] * 4 + [hbm] + [vmem] * 2,
        out_specs=(vmem,) * 4,
        scratch_shapes=[
            pltpu.VMEM((experts, tok_rows, features + 128), jnp.bfloat16),
            pltpu.VMEM((units, features), jnp.bfloat16),
            pltpu.VMEM((slots, features), jnp.bfloat16),
            pltpu.VMEM((experts * tok_rows, experts * tok_rows), jnp.bfloat16),
            pltpu.VMEM((experts, 8, 128), jnp.float32),
            pltpu.VMEM((experts, 8, 128), jnp.float32),
            dma,
            dma((experts,)),
            dma((experts,)),
            dma((experts,)),
            dma((experts,)),
        ],
        compiler_params=pltpu.CompilerParams(
            collective_id=0, has_side_effects=True, vmem_limit_bytes=56 * 1024 * 1024
        ),
    )(routes.T, gates.T, grad_out, hidden[0, 0], down_weight[0], adapter_a[0], adapter_b[0])
    grad_hid, grad_gates, grad_a, grad_b = pl.pallas_call(
        copy_kernel,
        out_shape=out_shape,
        in_specs=[vmem] * 4,
        out_specs=(vmem,) * 4,
        compiler_params=pltpu.CompilerParams(vmem_limit_bytes=60 * 1024 * 1024),
    )(*results)
    return grad_hid[None, None], grad_gates.T, grad_a[None], grad_b[None]


def solution(mesh):
    placed = (
        P(("job", "dp", "expert"), None),
        P(("job", "dp", "expert"), None),
        P(("job", "dp", "expert"), None),
        P("expert", ("job", "dp"), None, None),
        P("expert", "dp", None),
        P(("job", "expert"), None, None),
        P(("job", "expert"), None, None),
    )
    experts = mesh.shape["expert"]
    fused = mesh.shape["dp"] == 1 and experts == 16
    return jax.shard_map(
        functools.partial(fused_shards, experts) if fused else shards,
        mesh=mesh,
        in_specs=placed,
        out_specs=(
            P("expert", ("job", "dp"), None, None),
            P(("job", "dp", "expert"), None),
            P(("job", "expert"), None, None),
            P(("job", "expert"), None, None),
        ),
        check_vma=False,
    )
```

```python
import functools

import jax
import jax.numpy as jnp
from jax import lax
from jax.experimental import pallas as pl
from jax.experimental.pallas import tpu as pltpu
from jax.sharding import PartitionSpec as P

ADAPTER_SCALING = 1.0
MESH = pl.DeviceIdType.MESH


def contract_product(left, right, left_dim, right_dim):
    return lax.dot_general(
        left, right, (((left_dim,), (right_dim,)), ((), ())), preferred_element_type=jnp.float32
    )


def expert_terms(
    frozen_gradient_term,
    grad_rows,
    gate_rows,
    hidden_slot_rows,
    adapter_down_factor,
    factor_b,
    gate_scaled_rows,
):
    lowrank_backward = contract_product(grad_rows, factor_b, 1, 1)
    passed_gradient = frozen_gradient_term + ADAPTER_SCALING * jnp.dot(
        lowrank_backward.astype(jnp.bfloat16),
        adapter_down_factor,
        preferred_element_type=jnp.float32,
    )
    grad_hid = (gate_rows[:, None] * passed_gradient).astype(jnp.bfloat16)
    slot_dgate = jnp.sum(hidden_slot_rows.astype(jnp.float32) * passed_gradient, axis=1)
    gate_weighted_output = (gate_rows[:, None] * lowrank_backward).astype(jnp.bfloat16)
    first_factor_term = ADAPTER_SCALING * contract_product(
        gate_weighted_output, hidden_slot_rows, 0, 0
    )
    lowrank_forward = contract_product(hidden_slot_rows, adapter_down_factor, 1, 1).astype(
        jnp.bfloat16
    )
    second_factor_term = ADAPTER_SCALING * contract_product(lowrank_forward, gate_scaled_rows, 0, 0)
    return (grad_hid, slot_dgate, first_factor_term, second_factor_term)


def shards(routes, gates, grad_out, hidden, down_weight, adapter_a, adapter_b):
    tok_rows, top_count = routes.shape
    experts = lax.axis_size("expert")
    slots = hidden.shape[2]
    capacity = slots // experts
    per_block = tok_rows * top_count
    chosen = routes.reshape(per_block)
    onehot = (chosen[:, None] == jnp.arange(experts, dtype=jnp.int32)[None, :]).astype(jnp.int32)
    position = jnp.sum((jnp.cumsum(onehot, axis=0) - onehot) * onehot, axis=1)
    slot_of = chosen * capacity + position
    placing = slot_of[:, None] == jnp.arange(slots, dtype=jnp.int32)[None, :]
    tok_place = jnp.any(placing.reshape(tok_rows, top_count, slots), axis=1).astype(jnp.bfloat16)
    send_grad = (
        contract_product(tok_place, grad_out, 0, 0)
        .astype(jnp.bfloat16)
        .reshape(experts, capacity, grad_out.shape[1])
    )
    send_gate = jnp.sum(jnp.where(placing, gates.reshape(per_block)[:, None], 0.0), axis=0).reshape(
        experts, capacity
    )
    recv_grad, recv_gate = (
        lax.all_to_all(send_grad, "expert", split_axis=0, concat_axis=0, tiled=True),
        lax.all_to_all(
            send_gate.astype(jnp.bfloat16), "expert", split_axis=0, concat_axis=0, tiled=True
        ).astype(send_gate.dtype),
    )
    grad_rows = recv_grad.reshape(slots, grad_out.shape[1])
    gate_rows = recv_gate.reshape(slots)
    hidden_slot_rows = hidden[0, 0]
    adapter_down_factor = adapter_a[0]
    factor_b = adapter_b[0]
    gate_scaled_rows = (gate_rows[:, None] * grad_rows.astype(jnp.float32)).astype(jnp.bfloat16)
    frozen_gradient_term = contract_product(
        grad_rows, lax.all_gather(down_weight[0], "dp", axis=0, tiled=True), 1, 1
    )
    grad_hid, slot_dgate, first_factor_term, second_factor_term = expert_terms(
        frozen_gradient_term,
        grad_rows,
        gate_rows,
        hidden_slot_rows,
        adapter_down_factor,
        factor_b,
        gate_scaled_rows,
    )
    gradient_first_factor, gradient_second_factor = (
        lax.psum(first_factor_term.astype(jnp.bfloat16), "dp").astype(jnp.float32),
        lax.psum(second_factor_term.astype(jnp.bfloat16), "dp").astype(jnp.float32),
    )
    back_gate = lax.all_to_all(
        slot_dgate.reshape(experts, capacity), "expert", split_axis=0, concat_axis=0, tiled=True
    )
    grad_gates = jnp.sum(
        jnp.where(placing, back_gate.reshape(slots)[None, :], 0.0), axis=1
    ).reshape(tok_rows, top_count)
    return (
        grad_hid[None, None],
        grad_gates,
        gradient_first_factor[None],
        gradient_second_factor[None],
    )


def flip(value, bit):
    return value + bit - 2 * bit * ((value // bit) % 2)


def xor(value, mask):
    bit = 1
    while bit <= mask:
        if mask & bit:
            value = flip(value, bit)
        bit *= 2
    return value


def one_hot(shape, pick):
    rows = lax.broadcasted_iota(jnp.int32, shape, 0)
    columns = lax.broadcasted_iota(jnp.int32, shape, 1)
    return pick(rows, columns).astype(jnp.bfloat16)


def tile_of(size, most):
    tile = most
    while size % tile:
        tile //= 2
    return tile


def fused_kernel(
    experts,
    routes_ref,
    gates_ref,
    grad_ref,
    hidden_ref,
    weight_hbm,
    a_ref,
    b_ref,
    grad_hid_ref,
    grad_gates_ref,
    grad_a_ref,
    grad_b_ref,
    tokens,
    weight,
    rows,
    before,
    back_out,
    back_in,
    weight_sem,
    send_sem,
    recv_sem,
    back_send_sem,
    back_recv_sem,
):
    me = lax.axis_index("expert")
    top_count, tok_rows = routes_ref.shape
    features = grad_ref.shape[1]
    slots, units = hidden_ref.shape
    capacity = slots // experts
    total = experts * tok_rows
    planes = experts // 4
    z, x, core = me // 4, (me // 2) % 2, me % 2
    bf16, f32 = jnp.bfloat16, jnp.float32

    load_weight = pltpu.make_async_copy(weight_hbm, weight, weight_sem)
    load_weight.start()

    barrier = pltpu.get_barrier_semaphore()
    for step in range(1, experts):
        pl.semaphore_signal(
            barrier,
            inc=1,
            device_id={"expert": lax.rem(me + step, experts)},
            device_id_type=MESH,
        )

    def place_of(plane, column, lane):
        return (column * 2 + lane) * planes + plane

    own = place_of(z, x, core)
    tokens[own, :, :features] = grad_ref[...]
    high = gates_ref[...].astype(bf16)
    low = (gates_ref[...] - high.astype(f32)).astype(bf16)
    meta = jnp.zeros((tok_rows, 128), f32)
    for part, values in enumerate((routes_ref[...].astype(f32).astype(bf16), high, low)):
        spread = one_hot((top_count, 128), lambda r, c: c == r + part * top_count)
        meta = meta + contract_product(values, spread, 0, 0)
    tokens[own, :, features:] = meta.astype(bf16)
    pl.semaphore_wait(barrier, experts - 1)

    def source_of(token):
        stored = lax.div(token, tok_rows)
        return lax.rem(stored, planes) * 4 + lax.div(stored, planes)

    def index(plane, column, lane):
        return plane * 4 + column * 2 + lane

    x_mate, core_mate = index(z, 1 - x, core), index(z, x, 1 - core)
    sent = []

    def held(first, count):
        return tokens.at[pl.ds(first, count)]

    def send(first, count, target):
        copy = pltpu.make_async_remote_copy(
            src_ref=held(first, count),
            dst_ref=held(first, count),
            send_sem=send_sem.at[len(sent)],
            recv_sem=recv_sem.at[first],
            device_id={"expert": target},
            device_id_type=MESH,
        )
        copy.start()
        sent.append(copy)

    def arrived(first, count):
        pltpu.make_async_remote_copy(
            src_ref=held(first, count),
            dst_ref=held(first, count),
            send_sem=send_sem.at[0],
            recv_sem=recv_sem.at[first],
            device_id={"expert": core_mate},
            device_id_type=MESH,
        ).wait_recv()

    near, far = 2 * (z // 2), 2 * (1 - z // 2)
    send(own, 1, index(xor(z, 2), x, core))
    send(own, 1, x_mate)
    for step in (1, 3):
        send(own, 1, index(xor(z, step), x, core))

    before[...] = one_hot(
        (total, total), lambda r, c: (r < c) & (lax.div(r, tok_rows) == lax.div(c, tok_rows))
    )
    low_fwd = contract_product(hidden_ref[...], a_ref[...], 1, 1)
    beside = place_of(xor(z, 1), x, core)
    arrived(beside, 1)
    send(beside, 1, x_mate)
    send(place_of(near, x, core), 2, core_mate)
    arrived(place_of(z, 1 - x, core), 1)
    for step in (2, 3):
        distant = place_of(xor(z, step), x, core)
        arrived(distant, 1)
        send(distant, 1, x_mate)
    send(place_of(far, x, core), 2, core_mate)
    arrived(place_of(xor(z, 1), 1 - x, core), 1)
    send(place_of(near, 1 - x, core), 2, core_mate)
    for step in (2, 3):
        arrived(place_of(xor(z, step), 1 - x, core), 1)
    send(place_of(far, 1 - x, core), 2, core_mate)
    for column in (x, 1 - x):
        for pair in (near, far):
            arrived(place_of(pair, column, 1 - core), 2)

    gathered = tokens[:, :, features:].reshape(total, 128)
    eye = one_hot((128, 128), lambda r, c: r == c)
    turned = contract_product(eye, gathered, 1, 1)
    named = turned[:top_count] == me.astype(f32)
    gate_of = jnp.where(
        named, turned[top_count : 2 * top_count] + turned[2 * top_count : 3 * top_count], 0.0
    )
    gate_tok = jnp.sum(gate_of, axis=0, keepdims=True)
    match = jnp.sum(named.astype(f32), axis=0, keepdims=True)
    position = contract_product(
        jnp.broadcast_to(match, (8, total)).astype(bf16), before[...], 1, 0
    )[:1]
    block = source_of(lax.broadcasted_iota(jnp.int32, (1, total), 1))
    slot_of = jnp.where(match > 0.0, block.astype(f32) * capacity + position, -1.0)
    slot_ids = lax.broadcasted_iota(jnp.int32, (slots, total), 0).astype(f32)
    placing = slot_ids == slot_of
    gate = jnp.sum(jnp.where(placing, gate_tok, 0.0), axis=1, keepdims=True)
    place = placing.astype(bf16)

    wide = tile_of(features, 512)
    for start in range(0, features, wide):
        columns = slice(start, start + wide)
        rows[:, columns] = contract_product(
            place, tokens[:, :, columns].reshape(total, wide), 1, 0
        ).astype(bf16)
    low_back = contract_product(rows[...], b_ref[...], 1, 1)
    low_back_b = low_back.astype(bf16)
    load_weight.wait()
    deep = tile_of(units, 256)
    dgate = jnp.zeros((slots, 1), f32)
    for start in range(0, units, deep):
        span = slice(start, start + deep)
        through = contract_product(rows[...], weight[span, :], 1, 1)
        through = through + contract_product(low_back_b, a_ref[:, span], 1, 0)
        grad_hid_ref[:, span] = (gate * through).astype(bf16)
        dgate = dgate + jnp.sum(hidden_ref[:, span].astype(f32) * through, axis=1, keepdims=True)

    dgate_tok = jnp.sum(jnp.where(placing, dgate, 0.0), axis=0, keepdims=True)
    exact = lax.Precision.HIGHEST
    source = lax.broadcasted_iota(jnp.int32, (experts, total), 0)
    owner = source_of(lax.broadcasted_iota(jnp.int32, (experts, total), 1))
    by_source = lax.dot_general(
        jnp.where(source == owner, dgate_tok, 0.0),
        one_hot((total, 128), lambda r, c: lax.rem(r, tok_rows) == c).astype(f32),
        (((1,), (0,)), ((), ())),
        precision=exact,
        preferred_element_type=f32,
    )
    back_out[...] = jnp.broadcast_to(by_source[:, None, :], back_out.shape)
    returned = []
    for step in range(1, experts):
        target = lax.rem(me + step, experts)
        copy = pltpu.make_async_remote_copy(
            src_ref=back_out.at[target],
            dst_ref=back_in.at[me],
            send_sem=back_send_sem.at[step],
            recv_sem=back_recv_sem.at[me],
            device_id={"expert": target},
            device_id_type=MESH,
        )
        copy.start()
        returned.append(copy)
    back_in[me] = back_out[me]

    weighted = (gate * low_back).astype(bf16)
    grad_a_ref[...] = contract_product(weighted, hidden_ref[...], 0, 0)
    scaled = (gate * low_fwd).astype(bf16)
    for start in range(0, features, wide):
        columns = slice(start, start + wide)
        grad_b_ref[:, columns] = contract_product(scaled, rows[:, columns], 0, 0)

    for copy in sent:
        copy.wait_send()
    for copy in returned:
        copy.wait_send()
    for step in range(1, experts):
        origin = lax.rem(me + step, experts)
        pltpu.make_async_remote_copy(
            src_ref=back_out.at[origin],
            dst_ref=back_in.at[origin],
            send_sem=back_send_sem.at[step],
            recv_sem=back_recv_sem.at[origin],
            device_id={"expert": origin},
            device_id_type=MESH,
        ).wait_recv()
    back = lax.dot_general(
        back_in[:, 0, :],
        one_hot((128, tok_rows), lambda r, c: r == c).astype(f32),
        (((1,), (0,)), ((), ())),
        precision=exact,
        preferred_element_type=f32,
    )
    chosen = routes_ref[...]
    picked = jnp.zeros((top_count, tok_rows), f32)
    for expert in range(experts):
        picked = picked + jnp.where(chosen == expert, back[expert : expert + 1, :], 0.0)
    grad_gates_ref[...] = picked


def copy_kernel(*refs):
    count = len(refs) // 2
    for i in range(count):
        refs[count + i][...] = refs[i][...]


def fused_shards(experts, routes, gates, grad_out, hidden, down_weight, adapter_a, adapter_b):
    tok_rows, top_count = routes.shape
    features = grad_out.shape[1]
    slots, units = hidden.shape[2:]
    vmem = pl.BlockSpec(memory_space=pltpu.VMEM)
    hbm = pl.BlockSpec(memory_space=pl.ANY)
    dma = pltpu.SemaphoreType.DMA
    out_shape = (
        jax.ShapeDtypeStruct((slots, units), jnp.bfloat16),
        jax.ShapeDtypeStruct((top_count, tok_rows), jnp.float32),
        jax.ShapeDtypeStruct(adapter_a.shape[1:], jnp.float32),
        jax.ShapeDtypeStruct(adapter_b.shape[1:], jnp.float32),
    )
    results = pl.pallas_call(
        functools.partial(fused_kernel, experts),
        out_shape=out_shape,
        in_specs=[vmem] * 4 + [hbm] + [vmem] * 2,
        out_specs=(vmem,) * 4,
        scratch_shapes=[
            pltpu.VMEM((experts, tok_rows, features + 128), jnp.bfloat16),
            pltpu.VMEM((units, features), jnp.bfloat16),
            pltpu.VMEM((slots, features), jnp.bfloat16),
            pltpu.VMEM((experts * tok_rows, experts * tok_rows), jnp.bfloat16),
            pltpu.VMEM((experts, 8, 128), jnp.float32),
            pltpu.VMEM((experts, 8, 128), jnp.float32),
            dma,
            dma((experts,)),
            dma((experts,)),
            dma((experts,)),
            dma((experts,)),
        ],
        compiler_params=pltpu.CompilerParams(
            collective_id=0, has_side_effects=True, vmem_limit_bytes=56 * 1024 * 1024
        ),
    )(routes.T, gates.T, grad_out, hidden[0, 0], down_weight[0], adapter_a[0], adapter_b[0])
    grad_hid, grad_gates, grad_a, grad_b = pl.pallas_call(
        copy_kernel,
        out_shape=out_shape,
        in_specs=[vmem] * 4,
        out_specs=(vmem,) * 4,
        compiler_params=pltpu.CompilerParams(vmem_limit_bytes=60 * 1024 * 1024),
    )(*results)
    return grad_hid[None, None], grad_gates.T, grad_a[None], grad_b[None]


def solution(mesh):
    placed = (
        P(("job", "dp", "expert"), None),
        P(("job", "dp", "expert"), None),
        P(("job", "dp", "expert"), None),
        P("expert", ("job", "dp"), None, None),
        P("expert", "dp", None),
        P(("job", "expert"), None, None),
        P(("job", "expert"), None, None),
    )
    experts = mesh.shape["expert"]
    fused = mesh.shape["dp"] == 1 and experts == 16
    return jax.shard_map(
        functools.partial(fused_shards, experts) if fused else shards,
        mesh=mesh,
        in_specs=placed,
        out_specs=(
            P("expert", ("job", "dp"), None, None),
            P(("job", "dp", "expert"), None),
            P(("job", "expert"), None, None),
            P(("job", "expert"), None, None),
        ),
        check_vma=False,
    )
```
